1024 devices in a mesh: dp: 16 (over x, y), fsdp: 16 (over z_lo, core), seq: 4 (over z_hi).
Axes of the slice: x: 4, y: 4, z: 32 (z_hi: 4, z_lo: 8; z = z_hi * 8 + z_lo), core: 2. Of those that a mesh axis runs over, the one named last changes fastest.
Arguments:
- tokens: bfloat16 [256, 2048, 3200], P(('dp', 'fsdp'), 'seq'), may hold values from -300 to 300
- query: bfloat16 [16, 200], replicated, may hold values from -4 to 4
- value_weight: bfloat16 [3200, 768], P('fsdp'), may hold values from -0.109375 to 0.109375
- frames: int32 [256], P(('dp', 'fsdp')), may hold values from 4 to 16
- text_feat: float32 [256, 768], P(('dp', 'fsdp')), may hold values from -6 to 6
- pair: int32 [256], replicated, may hold values from 0 to 255, each once
- logit_scale: float32 [], replicated, may hold values from 10 to 60
Outputs:
- video_embed: float32 [256, 768], P(('dp', 'fsdp'))
- grad_video: float32 [256, 768], P(('dp', 'fsdp'))
- grad_text: float32 [256, 768], P(('dp', 'fsdp'))
- loss: float32 [], replicated
The draws below stay inside these ranges and needn't reach their ends.
All inputs are finite; a program needn't handle non-finite values.
Results may differ from the reference program's by a relative error of at most 0.0003.
Values may be sent and summed in bfloat16 or wider, within the bound.
No kernel may reach another device: no remote copies, remote signals or barrier semaphores. Data moves between devices by JAX's collectives and lax.ppermute only.
A program may use at most 32 MiB of HBM per device.

```python
import math
import jax
import jax.numpy as jnp
from jax import lax

D = 3200
E = 768
H = 16
FT = 128
FRAMES = 16
CLIPS = 256


def shared_query(key):
    return jnp.clip(jax.random.normal(key, (H, D // H), jnp.float32), -4.0, 4.0)


def draw_query(key, part):
    return shared_query(key).astype(jnp.bfloat16)


def planted(base, q_rows, key_pos, key_level, height):
    count = FRAMES * FT
    offsets = jax.random.randint(key_pos, (CLIPS, 3), 0, FT)
    places = offsets + FT * jnp.arange(3, dtype=jnp.int32)[None, :]
    level = jax.random.randint(key_level, (CLIPS,), 0, 3).astype(jnp.float32)
    peak = level * height
    strengths = jnp.stack([peak, peak + 2.0, 0.5 * peak], axis=1) / jnp.sqrt(jnp.float32(D // H))
    target = q_rows.reshape(1, 1, D)
    spots = jnp.arange(count, dtype=jnp.int32)[None, :, None] == places[:, None, :]
    chosen = jnp.sum(spots.astype(jnp.float32) * strengths[:, None, :], axis=2)
    hit = jnp.sum(spots.astype(jnp.float32), axis=2) > 0.5
    aligned = chosen[:, :, None] * target + 0.3 * base
    return jnp.where(hit[:, :, None], aligned, base)


def draw_tokens(key, part):
    q_rows = shared_query(key)
    key = jax.random.fold_in(key, 3)
    key_base = jax.random.fold_in(key, 0)
    key_pos = jax.random.fold_in(key, 1)
    key_level = jax.random.fold_in(key, 3)
    count = FRAMES * FT
    base = jnp.clip(jax.random.normal(key_base, (CLIPS, count, D), jnp.float32), -6.0, 6.0)
    base = planted(base, q_rows, key_pos, key_level, 110.0)
    return base.astype(jnp.bfloat16)


def set_ends(values, stream_key, smallest, largest):
    shape = values.shape
    place = [jax.random.randint(jax.random.fold_in(stream_key, axis), (), 0, shape[axis]) for axis in range(len(shape))]
    values = values.at[tuple(place)].set(smallest)
    longest = shape.index(max(shape))
    place[longest] = (place[longest] + 1) % shape[longest]
    return values.at[tuple(place)].set(largest)


def shard_levels(stream_key, extent, shards, smallest, top_value):
    loudness, own = 1.0, jax.random.fold_in(stream_key, 6)
    for dim, blocks in shards:
        heights = jnp.exp(jax.random.uniform(jax.random.fold_in(own, dim), (blocks,), jnp.float32, smallest / len(shards), top_value / len(shards)))
        loudness = loudness * jnp.repeat(heights, extent[dim] // blocks).reshape([-1 if axis == dim else 1 for axis in range(len(extent))])
    return loudness


def scatter_about(rng, shape, scale, most, pieces=(), kind=jnp.bfloat16):
    drawn = jax.random.normal(rng, shape, jnp.float32) * scale
    if len(pieces) > 0:
        drawn = shard_levels(rng, shape, pieces, -0.22, 0.18) * drawn
    return jnp.clip(drawn, min=-most, max=most).astype(kind)


def setup_inputs(seed: int = 0) -> dict:
    key_of = jax.random.split(jax.random.key(seed), 8)
    return {
        "tokens": draw_tokens(jax.random.fold_in(key_of[7], 71), 0),
        "query": draw_query(jax.random.fold_in(key_of[7], 71), 0),
        "value_weight": scatter_about(key_of[2], (D, E), D ** -0.5, 0.109375, ((0, 16),)),
        "frames": set_ends(jax.random.randint(key_of[3], (CLIPS,), 4, 17), jax.random.fold_in(key_of[3], 1), 4, 16).astype(jnp.int32),
        "text_feat": scatter_about(key_of[4], (CLIPS, E), 1.0, 6.0, ((0, 256),), jnp.float32),
        "pair": jax.random.permutation(key_of[5], CLIPS).astype(jnp.int32),
        "logit_scale": jnp.clip(jnp.exp(jax.random.uniform(key_of[6], (), jnp.float32, math.log(10.0), math.log(60.0))), 10.0, 60.0),
    }


def pool_clip(inputs, query, value_weight):
    clip_tokens, clip_frames = inputs
    count = clip_tokens.shape[0]
    heads = query.shape[0]
    slice_w = query.shape[1]
    xs = clip_tokens.astype(jnp.float32)
    scores = jnp.einsum('thd,hd->th', xs.reshape(count, heads, slice_w), query.astype(jnp.float32), precision=lax.Precision.HIGHEST) / jnp.sqrt(jnp.float32(slice_w))
    valid = jnp.arange(count, dtype=jnp.int32) // FT < clip_frames
    scores = jnp.where(valid[:, None], scores, jnp.float32(-1e+30))
    top = lax.optimization_barrier(jnp.max(scores, axis=0))
    expd = jnp.where(valid[:, None], jnp.exp(scores - top[None, :]), jnp.float32(0.0))
    weights = expd / lax.optimization_barrier(jnp.sum(expd, axis=0))[None, :]
    mixed = jnp.einsum('th,td->hd', weights, xs, precision=lax.Precision.HIGHEST)
    wslab = value_weight.astype(jnp.float32).reshape(value_weight.shape[0], heads, -1)
    pooled = jnp.einsum('hd,dhe->he', mixed, wslab, precision=lax.Precision.HIGHEST)
    return pooled.reshape(-1)

def unit_rows(values):
    return values * lax.rsqrt(lax.optimization_barrier(jnp.sum(values * values, axis=1, keepdims=True)) + 1e-06)

def reference(tokens, query, value_weight, frames, text_feat, pair, logit_scale):
    pooled = lax.map(lambda item: pool_clip(item, query, value_weight), (tokens, frames))
    video_embed = unit_rows(pooled)
    text_unit = unit_rows(text_feat)
    count = video_embed.shape[0]
    logits = logit_scale * jnp.dot(video_embed, text_unit.T, precision=lax.Precision.HIGHEST)
    row_top = lax.optimization_barrier(jnp.max(logits, axis=1))
    row_lse = row_top + jnp.log(lax.optimization_barrier(jnp.sum(jnp.exp(logits - row_top[:, None]), axis=1)))
    col_top = lax.optimization_barrier(jnp.max(logits, axis=0))
    col_lse = col_top + jnp.log(lax.optimization_barrier(jnp.sum(jnp.exp(logits - col_top[None, :]), axis=0)))
    onehot = pair[:, None] == jnp.arange(count, dtype=jnp.int32)[None, :]
    positive = lax.optimization_barrier(jnp.sum(jnp.where(onehot, logits, jnp.float32(0.0)), axis=1))
    loss = (jnp.sum(row_lse) + jnp.sum(col_lse) - 2.0 * jnp.sum(positive)) / (2.0 * count)
    grad_logits = (jnp.exp(logits - row_lse[:, None]) + jnp.exp(logits - col_lse[None, :]) - 2.0 * onehot.astype(jnp.float32)) / (2.0 * count)
    grad_video = logit_scale * jnp.dot(grad_logits, text_unit, precision=lax.Precision.HIGHEST)
    grad_text = logit_scale * jnp.dot(grad_logits.T, video_embed, precision=lax.Precision.HIGHEST)
    return (video_embed, grad_video, grad_text, loss)
```

```python
import jax
import jax.numpy as jnp
from jax import lax
from jax.experimental import pallas as pl
from jax.experimental.pallas import tpu as pltpu
from jax.sharding import Mesh, PartitionSpec as P

D, E, H, FT = 3200, 768, 16, 128
W_H = D // H
W_E = E // H
CHUNKS = 16
ROWS = D // CHUNKS
TOK = 512
FRAMES_HERE = TOK // FT
HIGH = lax.Precision.HIGHEST
F32, BF16 = jnp.float32, jnp.bfloat16
VMEM_LIMIT = 40 * 1024 * 1024


def three_terms(value):
    first = value.astype(BF16)
    rest = value - first.astype(F32)
    second = rest.astype(BF16)
    third = (rest - second.astype(F32)).astype(BF16)
    return first, second, third


def pool_kernel(frames_ref, query_ref, tok_hbm, parts_ref, state_ref, tok, spread, mixed, sems):
    copies = [
        pltpu.make_async_copy(tok_hbm.at[0, pl.ds(FT * j, FT)], tok.at[pl.ds(FT * j, FT)], sems.at[j])
        for j in range(FRAMES_HERE)
    ]
    for copy in copies:
        copy.start()
    spread[...] = jnp.zeros_like(spread)
    rows = query_ref[...].astype(F32)
    for h in range(H):
        spread[h : h + 1, W_H * h : W_H * (h + 1)] = rows[h : h + 1, :]
    heads_q = spread[...].astype(BF16)
    used = frames_ref[0] - lax.axis_index("s") * FRAMES_HERE
    scores = []
    for j in range(FRAMES_HERE):
        copies[j].wait()
        part = lax.dot_general(
            heads_q, tok[FT * j : FT * (j + 1), :], (((1,), (1,)), ((), ())), preferred_element_type=F32
        )
        scores.append(jnp.where(j < used, part * F32(W_H**-0.5), F32(-1e30)))
    score = jnp.concatenate(scores, axis=1)
    top = jnp.max(score, axis=1, keepdims=True)
    frame = lax.broadcasted_iota(jnp.int32, (H, TOK), 1) // FT
    expd = jnp.where(frame < used, jnp.exp(score - top), F32(0.0))
    total = jnp.sum(expd, axis=1, keepdims=True)
    terms = jnp.concatenate(three_terms(expd), axis=0)
    step = 640
    for n in range(D // step):
        cols = slice(step * n, step * (n + 1))
        out = jnp.dot(terms, tok[:, cols], preferred_element_type=F32)
        mixed[:, cols] = (out[2 * H :] + out[H : 2 * H]) + out[:H]
    for k in range(CHUNKS):
        parts_ref[k, :, 0:ROWS] = mixed[:, ROWS * k : ROWS * (k + 1)]
    lane = lax.broadcasted_iota(jnp.int32, (H, 128), 1)
    head = lax.broadcasted_iota(jnp.int32, (H, 128), 0)
    row = jnp.where(lane == 64 + head, top, 0.0) + jnp.where(lane == 80 + head, total, 0.0)
    state_ref[...] = jnp.broadcast_to(jnp.sum(row, axis=0, keepdims=True), (8, 128))


def pool(frames, query, tokens):
    return pl.pallas_call(
        pool_kernel,
        out_shape=(
            jax.ShapeDtypeStruct((CHUNKS, H, 256), F32),
            jax.ShapeDtypeStruct((8, 128), F32),
        ),
        in_specs=[
            pl.BlockSpec(memory_space=pltpu.SMEM),
            pl.BlockSpec(memory_space=pltpu.VMEM),
            pl.BlockSpec(memory_space=pl.ANY),
        ],
        out_specs=(pl.BlockSpec(memory_space=pltpu.VMEM), pl.BlockSpec(memory_space=pltpu.VMEM)),
        scratch_shapes=[
            pltpu.VMEM((TOK, D), BF16),
            pltpu.VMEM((H, D), F32),
            pltpu.VMEM((H, D), F32),
            pltpu.SemaphoreType.DMA((FRAMES_HERE,)),
        ],
        compiler_params=pltpu.CompilerParams(vmem_limit_bytes=VMEM_LIMIT),
        cost_estimate=pl.CostEstimate(flops=4 * 64 * TOK * D, bytes_accessed=TOK * D * 2, transcendentals=H * TOK),
        name="pool",
    )(frames, query, tokens)


def project_kernel(parts_ref, weight_ref, out_ref):
    x = parts_ref[...].reshape(CHUNKS * H, 256)[:, :ROWS]
    first, second, third = three_terms(x)
    weight = weight_ref[...]
    own = lax.broadcasted_iota(jnp.int32, (H, 256), 0)
    lane = lax.broadcasted_iota(jnp.int32, (H, 256), 1)
    for n in range(E // 256):
        w = weight[:, 256 * n : 256 * (n + 1)]
        y = jnp.dot(third, w, preferred_element_type=F32)
        y = y + jnp.dot(second, w, preferred_element_type=F32)
        y = y + jnp.dot(first, w, preferred_element_type=F32)
        mine = (lane + 256 * n) // W_E == own
        y = jnp.where(mine[None], y.reshape(CHUNKS, H, 256), 0.0)
        y = jnp.sum(y, axis=1)
        out_ref[:, 2 * n, :] = y[:, :128]
        out_ref[:, 2 * n + 1, :] = y[:, 128:]
    zero = jnp.zeros((CHUNKS, 128), F32)
    out_ref[:, 6, :] = zero
    out_ref[:, 7, :] = zero


def project(parts, weight):
    return pl.pallas_call(
        project_kernel,
        out_shape=jax.ShapeDtypeStruct((CHUNKS, 8, 128), F32),
        in_specs=[pl.BlockSpec(memory_space=pltpu.VMEM)] * 2,
        out_specs=pl.BlockSpec(memory_space=pltpu.VMEM),
        compiler_params=pltpu.CompilerParams(vmem_limit_bytes=VMEM_LIMIT),
        name="project",
    )(parts, weight)


def share_kernel(sums_ref, state_ref, text_ref, out_ref):
    total = jnp.sum(sums_ref[...], axis=0)
    text = text_ref[...]
    s = lax.axis_index("s")
    quarter = text[:, 0:192]
    for q in range(1, 4):
        quarter = jnp.where(s == q, text[:, 192 * q : 192 * (q + 1)], quarter)
    lane = lax.broadcasted_iota(jnp.int32, (1, 128), 1)
    tail = jnp.concatenate([quarter[:, 128:192], jnp.zeros((1, 64), F32)], axis=1)
    tail = jnp.where(lane < 64, tail, state_ref[0:1, :])
    row = lax.broadcasted_iota(jnp.int32, (8, 128), 0)
    block = jnp.where(row < 6, total, jnp.where(row == 6, quarter[:, 0:128], tail))
    out_ref[...] = jnp.broadcast_to(block[None], out_ref.shape)


def share(sums, state, text):
    return pl.pallas_call(
        share_kernel,
        out_shape=jax.ShapeDtypeStruct((32, 8, 128), F32),
        in_specs=[pl.BlockSpec(memory_space=pltpu.VMEM)] * 3,
        out_specs=pl.BlockSpec(memory_space=pltpu.VMEM),
        compiler_params=pltpu.CompilerParams(vmem_limit_bytes=VMEM_LIMIT),
        name="share",
    )(sums, state, text)


def unit_rows(values):
    return values * lax.rsqrt(jnp.sum(values * values, axis=1, keepdims=True) + 1e-06)


def merge_kernel(parts_ref, out_ref, video_ref, rows):
    ends = [parts_ref[8 * s : 8 * (s + 1), 7, :] for s in range(4)]
    tops = [end[:, 64 : 64 + H] for end in ends]
    totals = [end[:, 80 : 80 + H] for end in ends]
    top = jnp.maximum(jnp.maximum(tops[0], tops[1]), jnp.maximum(tops[2], tops[3]))
    scales = [jnp.exp(t - top) for t in tops]
    total = sum(scale * value for scale, value in zip(scales, totals))
    scales = jnp.concatenate([scale / total for scale in scales], axis=0)
    lane = lax.broadcasted_iota(jnp.int32, (H, E), 1) // W_E
    head = lax.broadcasted_iota(jnp.int32, (H, E), 0)
    spread = jnp.where(lane == head, F32(1.0), F32(0.0))
    factors = jnp.dot(scales, spread, precision=HIGH, preferred_element_type=F32)
    pooled = jnp.zeros((8, E), F32)
    texts = []
    for s in range(4):
        mine = [parts_ref[8 * s : 8 * (s + 1), r, :] for r in range(6)]
        pooled = pooled + factors[8 * s : 8 * (s + 1)] * jnp.concatenate(mine, axis=1)
        texts += [parts_ref[8 * s : 8 * (s + 1), 6, :], ends[s][:, 0:64]]
    videos = unit_rows(pooled)
    texts = unit_rows(jnp.concatenate(texts, axis=1))
    out_ref[:, 0:8, :] = jnp.broadcast_to(videos[None], (16, 8, E))
    out_ref[:, 8:16, :] = jnp.broadcast_to(texts[None], (16, 8, E))
    rows[...] = videos
    video_ref[...] = rows[pl.ds(lax.axis_index("zl"), 1), :]


def merge(parts):
    return pl.pallas_call(
        merge_kernel,
        out_shape=(jax.ShapeDtypeStruct((16, 16, E), F32), jax.ShapeDtypeStruct((1, E), F32)),
        in_specs=[pl.BlockSpec(memory_space=pltpu.VMEM)],
        out_specs=(pl.BlockSpec(memory_space=pltpu.VMEM), pl.BlockSpec(memory_space=pltpu.VMEM)),
        scratch_shapes=[pltpu.VMEM((8, E), F32)],
        compiler_params=pltpu.CompilerParams(vmem_limit_bytes=VMEM_LIMIT),
        name="merge",
    )(parts)


def loss_kernel(scale_ref, pair_ref, mine_ref, other_ref, video_ref, text_ref, loss_ref, videos, texts, grads):
    core = lax.axis_index("c")
    here = lax.axis_index("xh") * 2 + lax.axis_index("xl")
    place = (here * 4 + lax.axis_index("y")) * 8 + lax.axis_index("zl")
    n = 256
    for ref, start in ((mine_ref, core * 128), (other_ref, (1 - core) * 128)):
        start = pl.multiple_of(start, 128)
        videos[pl.ds(start, 128), :] = ref[:, 0:8, :].reshape(128, E)
        texts[pl.ds(start, 128), :] = ref[:, 8:16, :].reshape(128, E)
    v, t = videos[...], texts[...]
    scale = scale_ref[0]
    logits = scale * lax.dot_general(
        v, t, (((1,), (1,)), ((), ())), precision=HIGH, preferred_element_type=F32
    )
    expd = jnp.exp(logits)
    row_sum = jnp.sum(expd, axis=1, keepdims=True)
    col_sum = jnp.sum(expd, axis=0, keepdims=True)
    row = lax.broadcasted_iota(jnp.int32, (n, n), 0)
    col = lax.broadcasted_iota(jnp.int32, (n, n), 1)
    row_id = 2 * (row % 128) + row // 128
    col_id = 2 * (col % 128) + col // 128
    pairs = jnp.sum(jnp.where(col == row_id, pair_ref[...].astype(F32), 0.0), axis=1, keepdims=True)
    hot = pairs == col_id.astype(F32)
    positive = jnp.sum(jnp.where(hot, logits, 0.0))
    loss_ref[0, 0] = (jnp.sum(jnp.log(row_sum)) + jnp.sum(jnp.log(col_sum)) - 2.0 * positive) / (2.0 * n)
    grad = (expd / row_sum + expd / col_sum - jnp.where(hot, F32(2.0), F32(0.0))) / (2.0 * n)
    grads[...] = grad
    own = core * 128 + place
    own_row = jnp.broadcast_to(grads[pl.ds(own, 1), :], (8, n))
    video_ref[...] = scale * jnp.dot(own_row, t, precision=HIGH, preferred_element_type=F32)[0:1, :]
    own_col = jnp.sum(jnp.where(col == own, grad, 0.0), axis=1, keepdims=True)
    text_ref[...] = scale * jnp.sum(own_col * v, axis=0, keepdims=True)


def losses(scale, pair, mine, other):
    vmem, smem = pl.BlockSpec(memory_space=pltpu.VMEM), pl.BlockSpec(memory_space=pltpu.SMEM)
    return pl.pallas_call(
        loss_kernel,
        out_shape=(
            jax.ShapeDtypeStruct((1, E), F32),
            jax.ShapeDtypeStruct((1, E), F32),
            jax.ShapeDtypeStruct((1, 1), F32),
        ),
        in_specs=[smem, vmem, vmem, vmem],
        out_specs=(vmem, vmem, smem),
        scratch_shapes=[pltpu.VMEM((256, E), F32), pltpu.VMEM((256, E), F32), pltpu.VMEM((256, 256), F32)],
        compiler_params=pltpu.CompilerParams(vmem_limit_bytes=VMEM_LIMIT),
        name="losses",
    )(scale, pair, mine, other)


def exchange(value, axes):
    return lax.all_to_all(value, axes, 0, 0, tiled=True)


def shards(tokens, query, value_weight, frames, text_feat, pair, logit_scale):
    parts, state = pool(frames, query, tokens)
    parts = exchange(parts, ("zl", "c"))
    sums = exchange(project(parts, value_weight), ("zl", "c"))
    gathered = exchange(share(sums, state, text_feat), ("s", "zl"))
    block, video_embed = merge(gathered)
    mine = exchange(block, ("xh", "xl", "y"))
    other = lax.ppermute(mine, "c", [(0, 1), (1, 0)])
    grad_video, grad_text, loss = losses(logit_scale.reshape(1), pair.reshape(1, -1), mine, other)
    return (video_embed, grad_video, grad_text, loss.reshape(()))


def solution(mesh):
    axes = ("xh", "xl", "y", "zl", "c", "s")
    fine = Mesh(mesh.devices.reshape(2, 2, 4, 8, 2, 4), axes)
    clips = axes[:5]
    return jax.shard_map(
        shards,
        mesh=fine,
        in_specs=(
            P(clips, "s", None),
            P(),
            P(("zl", "c"), None),
            P(clips),
            P(clips, None),
            P(),
            P(),
        ),
        out_specs=(P(clips, None), P(clips, None), P(clips, None), P()),
        check_vma=False,
    )
```

```python
import jax
import jax.numpy as jnp
from jax import lax
from jax.experimental import pallas as pl
from jax.experimental.pallas import tpu as pltpu
from jax.sharding import Mesh, PartitionSpec as P

D, E, H, FT = 3200, 768, 16, 128
W_H = D // H
W_E = E // H
CHUNKS = 16
ROWS = D // CHUNKS
TOK = 512
FRAMES_HERE = TOK // FT
HIGH = lax.Precision.HIGHEST
F32, BF16 = jnp.float32, jnp.bfloat16
VMEM_LIMIT = 40 * 1024 * 1024
GROUP = ("xl", "y", "c")


def chunk_of(m, zl):
    return (((zl >> 2) ^ (zl & 1) ^ (m >> 2)) << 2) | ((zl ^ m) & 3)


def three_terms(value):
    first = value.astype(BF16)
    rest = value - first.astype(F32)
    second = rest.astype(BF16)
    third = (rest - second.astype(F32)).astype(BF16)
    return first, second, third


def pool_kernel(frames_ref, query_ref, tok_ref, parts_ref, state_ref, spread, mixed):
    tok = tok_ref.at[0]
    spread[...] = jnp.zeros_like(spread)
    rows = query_ref[...].astype(F32)
    for h in range(H):
        spread[h : h + 1, W_H * h : W_H * (h + 1)] = rows[h : h + 1, :]
    heads_q = spread[...].astype(BF16)
    used = frames_ref[0] - lax.axis_index("s") * FRAMES_HERE
    scores = []
    for j in range(FRAMES_HERE):
        part = lax.dot_general(
            heads_q, tok[FT * j : FT * (j + 1), :], (((1,), (1,)), ((), ())), preferred_element_type=F32
        )
        scores.append(jnp.where(j < used, part * F32(W_H**-0.5), F32(-1e30)))
    score = jnp.concatenate(scores, axis=1)
    top = jnp.max(score, axis=1, keepdims=True)
    frame = lax.broadcasted_iota(jnp.int32, (H, TOK), 1) // FT
    expd = jnp.where(frame < used, jnp.exp(score - top), F32(0.0))
    total = jnp.sum(expd, axis=1, keepdims=True)
    terms = jnp.concatenate(three_terms(expd), axis=0)
    step = 640
    for n in range(D // step):
        cols = slice(step * n, step * (n + 1))
        out = jnp.dot(terms, tok[:, cols], preferred_element_type=F32)
        mixed[:, cols] = (out[2 * H :] + out[H : 2 * H]) + out[:H]
    zl = lax.axis_index("zl")
    for k in range(CHUNKS):
        pair = k // 2
        member = (((pair >> 2) ^ (zl >> 2) ^ (zl & 1)) << 2) | ((pair ^ zl) & 3)
        parts_ref[2 * member + k % 2, :, 0:ROWS] = mixed[:, ROWS * k : ROWS * (k + 1)]
    lane = lax.broadcasted_iota(jnp.int32, (H, 128), 1)
    head = lax.broadcasted_iota(jnp.int32, (H, 128), 0)
    row = jnp.where(lane == 64 + head, top, 0.0) + jnp.where(lane == 80 + head, total, 0.0)
    state_ref[...] = jnp.broadcast_to(jnp.sum(row, axis=0, keepdims=True), (8, 128))


def pool(frames, query, tokens):
    return pl.pallas_call(
        pool_kernel,
        out_shape=(
            jax.ShapeDtypeStruct((CHUNKS, H, 256), F32),
            jax.ShapeDtypeStruct((8, 128), F32),
        ),
        in_specs=[
            pl.BlockSpec(memory_space=pltpu.SMEM),
            pl.BlockSpec(memory_space=pltpu.VMEM),
            pl.BlockSpec(memory_space=pltpu.VMEM),
        ],
        out_specs=(pl.BlockSpec(memory_space=pltpu.VMEM), pl.BlockSpec(memory_space=pltpu.VMEM)),
        scratch_shapes=[
            pltpu.VMEM((H, D), F32),
            pltpu.VMEM((H, D), F32),
        ],
        compiler_params=pltpu.CompilerParams(vmem_limit_bytes=VMEM_LIMIT),
        cost_estimate=pl.CostEstimate(flops=4 * 64 * TOK * D, bytes_accessed=TOK * D * 2, transcendentals=H * TOK),
        name="pool",
    )(frames, query, tokens)


def project_kernel(parts_ref, weight_ref, out_ref):
    x = parts_ref[...].reshape(CHUNKS * H, 256)[:, :ROWS]
    first, second, third = three_terms(x)
    weight = weight_ref[...]
    own = lax.broadcasted_iota(jnp.int32, (H, 256), 0)
    lane = lax.broadcasted_iota(jnp.int32, (H, 256), 1)
    for n in range(E // 256):
        w = weight[:, 256 * n : 256 * (n + 1)]
        y = jnp.dot(third, w, preferred_element_type=F32)
        y = y + jnp.dot(second, w, preferred_element_type=F32)
        y = y + jnp.dot(first, w, preferred_element_type=F32)
        mine = (lane + 256 * n) // W_E == own
        y = jnp.where(mine[None], y.reshape(CHUNKS, H, 256), 0.0)
        y = jnp.sum(y, axis=1)
        out_ref[:, 2 * n, :] = y[:, :128]
        out_ref[:, 2 * n + 1, :] = y[:, 128:]
    zero = jnp.zeros((CHUNKS, 128), F32)
    out_ref[:, 6, :] = zero
    out_ref[:, 7, :] = zero


def project(parts, weight):
    return pl.pallas_call(
        project_kernel,
        out_shape=jax.ShapeDtypeStruct((CHUNKS, 8, 128), F32),
        in_specs=[pl.BlockSpec(memory_space=pltpu.VMEM)] * 2,
        out_specs=pl.BlockSpec(memory_space=pltpu.VMEM),
        compiler_params=pltpu.CompilerParams(vmem_limit_bytes=VMEM_LIMIT),
        name="project",
    )(parts, weight)


def share_kernel(sums_ref, state_ref, out_ref):
    total = jnp.sum(sums_ref[...], axis=0)
    row = lax.broadcasted_iota(jnp.int32, (8, 128), 0)
    block = jnp.where(row < 6, total, state_ref[...])
    out_ref[...] = jnp.broadcast_to(block[None], out_ref.shape)


def share(sums, state):
    return pl.pallas_call(
        share_kernel,
        out_shape=jax.ShapeDtypeStruct((4, 8, 128), F32),
        in_specs=[pl.BlockSpec(memory_space=pltpu.VMEM)] * 2,
        out_specs=pl.BlockSpec(memory_space=pltpu.VMEM),
        compiler_params=pltpu.CompilerParams(vmem_limit_bytes=VMEM_LIMIT),
        name="share",
    )(sums, state)


def unit_rows(values):
    return values * lax.rsqrt(jnp.sum(values * values, axis=1, keepdims=True) + 1e-06)


def combine_kernel(parts_ref, text_ref, out_ref, video_ref):
    ends = parts_ref[:, 7, :]
    tops, totals = ends[:, 64 : 64 + H], ends[:, 80 : 80 + H]
    scales = jnp.exp(tops - jnp.max(tops, axis=0, keepdims=True))
    scales = scales / jnp.sum(scales * totals, axis=0, keepdims=True)
    lane = lax.broadcasted_iota(jnp.int32, (H, E), 1) // W_E
    head = lax.broadcasted_iota(jnp.int32, (H, E), 0)
    spread = jnp.where(lane == head, F32(1.0), F32(0.0))
    factors = jnp.dot(scales, spread, precision=HIGH, preferred_element_type=F32)
    values = jnp.concatenate([parts_ref[:, r, :] for r in range(6)], axis=1)
    video = unit_rows(jnp.sum(factors * values, axis=0, keepdims=True))
    video_ref[...] = video
    out_ref[:, 0, :] = jnp.broadcast_to(video, (8, E))
    out_ref[:, 1, :] = jnp.broadcast_to(unit_rows(text_ref[...]), (8, E))


def combine(parts, text):
    return pl.pallas_call(
        combine_kernel,
        out_shape=(jax.ShapeDtypeStruct((8, 2, E), F32), jax.ShapeDtypeStruct((1, E), F32)),
        in_specs=[pl.BlockSpec(memory_space=pltpu.VMEM)] * 2,
        out_specs=(pl.BlockSpec(memory_space=pltpu.VMEM), pl.BlockSpec(memory_space=pltpu.VMEM)),
        compiler_params=pltpu.CompilerParams(vmem_limit_bytes=VMEM_LIMIT),
        name="combine",
    )(parts, text)


def repeat_kernel(rows_ref, out_ref):
    out_ref[:, 0:8, :] = jnp.broadcast_to(rows_ref[:, 0, :][None], (16, 8, E))
    out_ref[:, 8:16, :] = jnp.broadcast_to(rows_ref[:, 1, :][None], (16, 8, E))


def repeat(rows):
    return pl.pallas_call(
        repeat_kernel,
        out_shape=jax.ShapeDtypeStruct((16, 16, E), F32),
        in_specs=[pl.BlockSpec(memory_space=pltpu.VMEM)],
        out_specs=pl.BlockSpec(memory_space=pltpu.VMEM),
        compiler_params=pltpu.CompilerParams(vmem_limit_bytes=VMEM_LIMIT),
        name="repeat",
    )(rows)


def loss_kernel(scale_ref, pair_ref, mine_ref, other_ref, video_ref, text_ref, loss_ref, videos, texts, grads):
    core = lax.axis_index("c")
    here = lax.axis_index("xh") * 2 + lax.axis_index("xl")
    place = (here * 4 + lax.axis_index("y")) * 8 + lax.axis_index("zl")
    n = 256
    for ref, start in ((mine_ref, core * 128), (other_ref, (1 - core) * 128)):
        start = pl.multiple_of(start, 128)
        videos[pl.ds(start, 128), :] = ref[:, 0:8, :].reshape(128, E)
        texts[pl.ds(start, 128), :] = ref[:, 8:16, :].reshape(128, E)
    v, t = videos[...], texts[...]
    scale = scale_ref[0]
    logits = scale * lax.dot_general(
        v, t, (((1,), (1,)), ((), ())), precision=HIGH, preferred_element_type=F32
    )
    expd = jnp.exp(logits)
    row_sum = jnp.sum(expd, axis=1, keepdims=True)
    col_sum = jnp.sum(expd, axis=0, keepdims=True)
    row = lax.broadcasted_iota(jnp.int32, (n, n), 0)
    col = lax.broadcasted_iota(jnp.int32, (n, n), 1)
    row_id = 2 * (row % 128) + row // 128
    col_id = 2 * (col % 128) + col // 128
    pairs = jnp.sum(jnp.where(col == row_id, pair_ref[...].astype(F32), 0.0), axis=1, keepdims=True)
    hot = pairs == col_id.astype(F32)
    positive = jnp.sum(jnp.where(hot, logits, 0.0))
    loss_ref[0, 0] = (jnp.sum(jnp.log(row_sum)) + jnp.sum(jnp.log(col_sum)) - 2.0 * positive) / (2.0 * n)
    grad = (expd / row_sum + expd / col_sum - jnp.where(hot, F32(2.0), F32(0.0))) / (2.0 * n)
    grads[...] = grad
    own = core * 128 + place
    own_row = jnp.broadcast_to(grads[pl.ds(own, 1), :], (8, n))
    video_ref[...] = scale * jnp.dot(own_row, t, precision=HIGH, preferred_element_type=F32)[0:1, :]
    own_col = jnp.sum(jnp.where(col == own, grad, 0.0), axis=1, keepdims=True)
    text_ref[...] = scale * jnp.sum(own_col * v, axis=0, keepdims=True)


def losses(scale, pair, mine, other):
    vmem, smem = pl.BlockSpec(memory_space=pltpu.VMEM), pl.BlockSpec(memory_space=pltpu.SMEM)
    return pl.pallas_call(
        loss_kernel,
        out_shape=(
            jax.ShapeDtypeStruct((1, E), F32),
            jax.ShapeDtypeStruct((1, E), F32),
            jax.ShapeDtypeStruct((1, 1), F32),
        ),
        in_specs=[smem, vmem, vmem, vmem],
        out_specs=(vmem, vmem, smem),
        scratch_shapes=[pltpu.VMEM((256, E), F32), pltpu.VMEM((256, E), F32), pltpu.VMEM((256, 256), F32)],
        compiler_params=pltpu.CompilerParams(vmem_limit_bytes=VMEM_LIMIT),
        name="losses",
    )(scale, pair, mine, other)


def exchange(value, axes):
    return lax.all_to_all(value, axes, 0, 0, tiled=True)


def shards(tokens, query, value_weight, frames, text_feat, pair, logit_scale):
    moves = [
        ((m * 8) + chunk_of(m, zl), m * 8 + zl)
        for m in range(8)
        for zl in range(8)
    ]
    weight = lax.ppermute(value_weight, ("xl", "y", "zl"), moves)
    parts, state = pool(frames, query, tokens)
    parts = exchange(parts, GROUP)
    sums = exchange(project(parts, weight), GROUP)
    rows, video_embed = combine(exchange(share(sums, state), "s"), text_feat)
    mine = exchange(repeat(exchange(rows, "zl")), ("xh", "xl", "y"))
    other = lax.ppermute(mine, "c", [(0, 1), (1, 0)])
    grad_video, grad_text, loss = losses(logit_scale.reshape(1), pair.reshape(1, -1), mine, other)
    return (video_embed, grad_video, grad_text, loss.reshape(()))


def solution(mesh):
    axes = ("xh", "xl", "y", "zl", "c", "s")
    fine = Mesh(mesh.devices.reshape(2, 2, 4, 8, 2, 4), axes)
    clips = axes[:5]
    return jax.shard_map(
        shards,
        mesh=fine,
        in_specs=(
            P(clips, "s", None),
            P(),
            P(("zl", "c"), None),
            P(clips),
            P(clips, None),
            P(),
            P(),
        ),
        out_specs=(P(clips, None), P(clips, None), P(clips, None), P()),
        check_vma=False,
    )
```

```python
import jax
import jax.numpy as jnp
from jax import lax
from jax.experimental import pallas as pl
from jax.experimental.pallas import tpu as pltpu
from jax.sharding import Mesh, PartitionSpec as P

D, E, H, FT = 3200, 768, 16, 128
W_H = D // H
W_E = E // H
CHUNKS = 16
ROWS = D // CHUNKS
TOK = 512
FRAMES_HERE = TOK // FT
HIGH = lax.Precision.HIGHEST
F32, BF16 = jnp.float32, jnp.bfloat16
VMEM_LIMIT = 40 * 1024 * 1024
POOL_LIMIT = 52 * 1024 * 1024
GROUP = ("xl", "y", "c")


def chunk_of(m, zl):
    return (((zl >> 2) ^ (zl & 1) ^ (m >> 2)) << 2) | ((zl ^ m) & 3)


def three_terms(value):
    first = value.astype(BF16)
    rest = value - first.astype(F32)
    second = rest.astype(BF16)
    third = (rest - second.astype(F32)).astype(BF16)
    return first, second, third


def pool_kernel(frames_ref, query_hbm, tok_hbm, parts_ref, state_ref, tok, query_ref, spread, mixed, sems):
    query_copy = pltpu.make_async_copy(query_hbm, query_ref, sems.at[FRAMES_HERE])
    query_copy.start()
    copies = [
        pltpu.make_async_copy(tok_hbm.at[0, pl.ds(FT * j, FT)], tok.at[pl.ds(FT * j, FT)], sems.at[j])
        for j in range(FRAMES_HERE)
    ]
    for copy in copies:
        copy.start()
    spread[...] = jnp.zeros_like(spread)
    query_copy.wait()
    rows = query_ref[...].astype(F32)
    for h in range(H):
        spread[h : h + 1, W_H * h : W_H * (h + 1)] = rows[h : h + 1, :]
    heads_q = spread[...].astype(BF16)
    used = frames_ref[0] - lax.axis_index("s") * FRAMES_HERE
    scores = []
    for j in range(FRAMES_HERE):
        copies[j].wait()
        part = lax.dot_general(
            heads_q, tok[FT * j : FT * (j + 1), :], (((1,), (1,)), ((), ())), preferred_element_type=F32
        )
        scores.append(jnp.where(j < used, part * F32(W_H**-0.5), F32(-1e30)))
    score = jnp.concatenate(scores, axis=1)
    top = jnp.max(score, axis=1, keepdims=True)
    frame = lax.broadcasted_iota(jnp.int32, (H, TOK), 1) // FT
    expd = jnp.where(frame < used, jnp.exp(score - top), F32(0.0))
    total = jnp.sum(expd, axis=1, keepdims=True)
    terms = jnp.concatenate(three_terms(expd), axis=0)
    step = 640
    for n in range(D // step):
        cols = slice(step * n, step * (n + 1))
        out = jnp.dot(terms, tok[:, cols], preferred_element_type=F32)
        mixed[:, cols] = (out[2 * H :] + out[H : 2 * H]) + out[:H]
    zl = lax.axis_index("zl")
    for k in range(CHUNKS):
        pair = k // 2
        member = (((pair >> 2) ^ (zl >> 2) ^ (zl & 1)) << 2) | ((pair ^ zl) & 3)
        parts_ref[2 * member + k % 2, :, 0:ROWS] = mixed[:, ROWS * k : ROWS * (k + 1)]
    lane = lax.broadcasted_iota(jnp.int32, (H, 128), 1)
    head = lax.broadcasted_iota(jnp.int32, (H, 128), 0)
    row = jnp.where(lane == 64 + head, top, 0.0) + jnp.where(lane == 80 + head, total, 0.0)
    state_ref[...] = jnp.broadcast_to(jnp.sum(row, axis=0, keepdims=True), (8, 128))


def pool(frames, query, tokens):
    return pl.pallas_call(
        pool_kernel,
        out_shape=(
            jax.ShapeDtypeStruct((CHUNKS, H, 256), F32),
            jax.ShapeDtypeStruct((8, 128), F32),
        ),
        in_specs=[
            pl.BlockSpec(memory_space=pltpu.SMEM),
            pl.BlockSpec(memory_space=pl.ANY),
            pl.BlockSpec(memory_space=pl.ANY),
        ],
        out_specs=(pl.BlockSpec(memory_space=pltpu.VMEM), pl.BlockSpec(memory_space=pltpu.VMEM)),
        scratch_shapes=[
            pltpu.VMEM((TOK, D), BF16),
            pltpu.VMEM((H, W_H), BF16),
            pltpu.VMEM((H, D), F32),
            pltpu.VMEM((H, D), F32),
            pltpu.SemaphoreType.DMA((FRAMES_HERE + 1,)),
        ],
        compiler_params=pltpu.CompilerParams(vmem_limit_bytes=POOL_LIMIT),
        cost_estimate=pl.CostEstimate(flops=4 * 64 * TOK * D, bytes_accessed=TOK * D * 2, transcendentals=H * TOK),
        name="pool",
    )(frames, query, tokens)


def project_kernel(parts_ref, weight_ref, out_ref):
    x = parts_ref[...].reshape(CHUNKS * H, 256)[:, :ROWS]
    first, second, third = three_terms(x)
    weight = weight_ref[...]
    own = lax.broadcasted_iota(jnp.int32, (H, 256), 0)
    lane = lax.broadcasted_iota(jnp.int32, (H, 256), 1)
    for n in range(E // 256):
        w = weight[:, 256 * n : 256 * (n + 1)]
        y = jnp.dot(third, w, preferred_element_type=F32)
        y = y + jnp.dot(second, w, preferred_element_type=F32)
        y = y + jnp.dot(first, w, preferred_element_type=F32)
        mine = (lane + 256 * n) // W_E == own
        y = jnp.where(mine[None], y.reshape(CHUNKS, H, 256), 0.0)
        y = jnp.sum(y, axis=1)
        out_ref[:, 2 * n, :] = y[:, :128]
        out_ref[:, 2 * n + 1, :] = y[:, 128:]
    zero = jnp.zeros((CHUNKS, 128), F32)
    out_ref[:, 6, :] = zero
    out_ref[:, 7, :] = zero


def project(parts, weight):
    return pl.pallas_call(
        project_kernel,
        out_shape=jax.ShapeDtypeStruct((CHUNKS, 8, 128), F32),
        in_specs=[pl.BlockSpec(memory_space=pltpu.VMEM)] * 2,
        out_specs=pl.BlockSpec(memory_space=pltpu.VMEM),
        compiler_params=pltpu.CompilerParams(vmem_limit_bytes=VMEM_LIMIT),
        name="project",
    )(parts, weight)


def share_kernel(sums_ref, state_ref, text_ref, out_ref):
    total = jnp.sum(sums_ref[...], axis=0)
    text = text_ref[...]
    s = lax.axis_index("s")
    quarter = text[:, 0:192]
    for q in range(1, 4):
        quarter = jnp.where(s == q, text[:, 192 * q : 192 * (q + 1)], quarter)
    lane = lax.broadcasted_iota(jnp.int32, (1, 128), 1)
    tail = jnp.concatenate([quarter[:, 128:192], jnp.zeros((1, 64), F32)], axis=1)
    tail = jnp.where(lane < 64, tail, state_ref[0:1, :])
    row = lax.broadcasted_iota(jnp.int32, (8, 128), 0)
    block = jnp.where(row < 6, total, jnp.where(row == 6, quarter[:, 0:128], tail))
    out_ref[...] = jnp.broadcast_to(block[None], out_ref.shape)


def share(sums, state, text):
    return pl.pallas_call(
        share_kernel,
        out_shape=jax.ShapeDtypeStruct((32, 8, 128), F32),
        in_specs=[pl.BlockSpec(memory_space=pltpu.VMEM)] * 3,
        out_specs=pl.BlockSpec(memory_space=pltpu.VMEM),
        compiler_params=pltpu.CompilerParams(vmem_limit_bytes=VMEM_LIMIT),
        name="share",
    )(sums, state, text)


def unit_rows(values):
    return values * lax.rsqrt(jnp.sum(values * values, axis=1, keepdims=True) + 1e-06)


def merge_kernel(parts_ref, out_ref, video_ref, rows):
    ends = [parts_ref[8 * s : 8 * (s + 1), 7, :] for s in range(4)]
    tops = [end[:, 64 : 64 + H] for end in ends]
    totals = [end[:, 80 : 80 + H] for end in ends]
    top = jnp.maximum(jnp.maximum(tops[0], tops[1]), jnp.maximum(tops[2], tops[3]))
    scales = [jnp.exp(t - top) for t in tops]
    total = sum(scale * value for scale, value in zip(scales, totals))
    scales = jnp.concatenate([scale / total for scale in scales], axis=0)
    lane = lax.broadcasted_iota(jnp.int32, (H, E), 1) // W_E
    head = lax.broadcasted_iota(jnp.int32, (H, E), 0)
    spread = jnp.where(lane == head, F32(1.0), F32(0.0))
    factors = jnp.dot(scales, spread, precision=HIGH, preferred_element_type=F32)
    pooled = jnp.zeros((8, E), F32)
    texts = []
    for s in range(4):
        mine = [parts_ref[8 * s : 8 * (s + 1), r, :] for r in range(6)]
        pooled = pooled + factors[8 * s : 8 * (s + 1)] * jnp.concatenate(mine, axis=1)
        texts += [parts_ref[8 * s : 8 * (s + 1), 6, :], ends[s][:, 0:64]]
    videos = unit_rows(pooled)
    texts = unit_rows(jnp.concatenate(texts, axis=1))
    out_ref[:, 0:8, :] = jnp.broadcast_to(videos[None], (16, 8, E))
    out_ref[:, 8:16, :] = jnp.broadcast_to(texts[None], (16, 8, E))
    rows[...] = videos
    video_ref[...] = rows[pl.ds(lax.axis_index("zl"), 1), :]


def merge(parts):
    return pl.pallas_call(
        merge_kernel,
        out_shape=(jax.ShapeDtypeStruct((16, 16, E), F32), jax.ShapeDtypeStruct((1, E), F32)),
        in_specs=[pl.BlockSpec(memory_space=pltpu.VMEM)],
        out_specs=(pl.BlockSpec(memory_space=pltpu.VMEM), pl.BlockSpec(memory_space=pltpu.VMEM)),
        scratch_shapes=[pltpu.VMEM((8, E), F32)],
        compiler_params=pltpu.CompilerParams(vmem_limit_bytes=VMEM_LIMIT),
        name="merge",
    )(parts)


def loss_kernel(scale_ref, pair_ref, mine_ref, other_ref, video_ref, text_ref, loss_ref, videos, texts, grads):
    core = lax.axis_index("c")
    here = lax.axis_index("xh") * 2 + lax.axis_index("xl")
    place = (here * 4 + lax.axis_index("y")) * 8 + lax.axis_index("zl")
    n = 256
    for ref, start in ((mine_ref, core * 128), (other_ref, (1 - core) * 128)):
        start = pl.multiple_of(start, 128)
        videos[pl.ds(start, 128), :] = ref[:, 0:8, :].reshape(128, E)
        texts[pl.ds(start, 128), :] = ref[:, 8:16, :].reshape(128, E)
    v, t = videos[...], texts[...]
    scale = scale_ref[0]
    logits = scale * lax.dot_general(
        v, t, (((1,), (1,)), ((), ())), precision=HIGH, preferred_element_type=F32
    )
    expd = jnp.exp(logits)
    row_sum = jnp.sum(expd, axis=1, keepdims=True)
    col_sum = jnp.sum(expd, axis=0, keepdims=True)
    row = lax.broadcasted_iota(jnp.int32, (n, n), 0)
    col = lax.broadcasted_iota(jnp.int32, (n, n), 1)
    row_id = 2 * (row % 128) + row // 128
    col_id = 2 * (col % 128) + col // 128
    pairs = jnp.sum(jnp.where(col == row_id, pair_ref[...].astype(F32), 0.0), axis=1, keepdims=True)
    hot = pairs == col_id.astype(F32)
    positive = jnp.sum(jnp.where(hot, logits, 0.0))
    loss_ref[0, 0] = (jnp.sum(jnp.log(row_sum)) + jnp.sum(jnp.log(col_sum)) - 2.0 * positive) / (2.0 * n)
    grad = (expd / row_sum + expd / col_sum - jnp.where(hot, F32(2.0), F32(0.0))) / (2.0 * n)
    grads[...] = grad
    own = core * 128 + place
    own_row = jnp.broadcast_to(grads[pl.ds(own, 1), :], (8, n))
    video_ref[...] = scale * jnp.dot(own_row, t, precision=HIGH, preferred_element_type=F32)[0:1, :]
    own_col = jnp.sum(jnp.where(col == own, grad, 0.0), axis=1, keepdims=True)
    text_ref[...] = scale * jnp.sum(own_col * v, axis=0, keepdims=True)


def losses(scale, pair, mine, other):
    vmem, smem = pl.BlockSpec(memory_space=pltpu.VMEM), pl.BlockSpec(memory_space=pltpu.SMEM)
    return pl.pallas_call(
        loss_kernel,
        out_shape=(
            jax.ShapeDtypeStruct((1, E), F32),
            jax.ShapeDtypeStruct((1, E), F32),
            jax.ShapeDtypeStruct((1, 1), F32),
        ),
        in_specs=[smem, vmem, vmem, vmem],
        out_specs=(vmem, vmem, smem),
        scratch_shapes=[pltpu.VMEM((256, E), F32), pltpu.VMEM((256, E), F32), pltpu.VMEM((256, 256), F32)],
        compiler_params=pltpu.CompilerParams(vmem_limit_bytes=VMEM_LIMIT),
        name="losses",
    )(scale, pair, mine, other)


def exchange(value, axes):
    return lax.all_to_all(value, axes, 0, 0, tiled=True)


def shards(tokens, query, value_weight, frames, text_feat, pair, logit_scale):
    moves = [
        ((m * 8) + chunk_of(m, zl), m * 8 + zl)
        for m in range(8)
        for zl in range(8)
    ]
    weight = lax.ppermute(value_weight, ("xl", "y", "zl"), moves)
    parts, state = pool(frames, query, tokens)
    parts = exchange(parts, GROUP)
    sums = exchange(project(parts, weight), GROUP)
    gathered = exchange(share(sums, state, text_feat), ("s", "zl"))
    block, video_embed = merge(gathered)
    mine = exchange(block, ("xh", "xl", "y"))
    other = lax.ppermute(mine, "c", [(0, 1), (1, 0)])
    grad_video, grad_text, loss = losses(logit_scale.reshape(1), pair.reshape(1, -1), mine, other)
    return (video_embed, grad_video, grad_text, loss.reshape(()))


def solution(mesh):
    axes = ("xh", "xl", "y", "zl", "c", "s")
    fine = Mesh(mesh.devices.reshape(2, 2, 4, 8, 2, 4), axes)
    clips = axes[:5]
    return jax.shard_map(
        shards,
        mesh=fine,
        in_specs=(
            P(clips, "s", None),
            P(),
            P(("zl", "c"), None),
            P(clips),
            P(clips, None),
            P(),
            P(),
        ),
        out_specs=(P(clips, None), P(clips, None), P(clips, None), P()),
        check_vma=False,
    )
```

```python
import jax
import jax.numpy as jnp
from jax import lax
from jax.experimental import pallas as pl
from jax.experimental.pallas import tpu as pltpu
from jax.sharding import Mesh, PartitionSpec as P

D, E, H, FT = 3200, 768, 16, 128
W_H = D // H
W_E = E // H
CHUNKS = 16
ROWS = D // CHUNKS
TOK = 512
FRAMES_HERE = TOK // FT
HIGH = lax.Precision.HIGHEST
F32, BF16 = jnp.float32, jnp.bfloat16
VMEM_LIMIT = 40 * 1024 * 1024
GROUP = ("xl", "y", "c")


PAIRS = (
    (3, 6, 1, 4, 0, 2, 5, 7),
    (5, 0, 4, 3, 7, 1, 6, 2),
    (0, 7, 3, 6, 1, 4, 2, 5),
    (4, 5, 2, 1, 6, 3, 7, 0),
    (1, 4, 7, 2, 5, 0, 3, 6),
    (6, 3, 0, 5, 2, 7, 4, 1),
    (2, 1, 6, 7, 4, 5, 0, 3),
    (7, 2, 5, 0, 3, 6, 1, 4),
)
HOPS = (
    (3, -3, -1, 1, 4, -3, -1, 0),
    (-3, -1, 2, 0, 3, -4, 0, 3),
    (0, -2, 1, 3, -3, -1, 4, -2),
    (4, -4, 0, -2, 2, -2, 1, 1),
    (1, 3, -3, -1, 1, 3, -3, -1),
    (-2, 2, -2, 2, -2, 2, -2, 2),
    (2, 0, 4, -4, 0, 0, 2, -4),
    (-1, 1, 3, -3, -1, 1, 3, -3),
)
MEMBERS = tuple(sum(m << (3 * PAIRS[m][zl]) for m in range(8)) for zl in range(8))


def three_terms(value):
    first = value.astype(BF16)
    rest = value - first.astype(F32)
    second = rest.astype(BF16)
    third = (rest - second.astype(F32)).astype(BF16)
    return first, second, third


def pool_kernel(frames_ref, query_ref, tok_ref, parts_ref, state_ref, spread, mixed):
    tok = tok_ref.at[0]
    spread[...] = jnp.zeros_like(spread)
    rows = query_ref[...].astype(F32)
    for h in range(H):
        spread[h : h + 1, W_H * h : W_H * (h + 1)] = rows[h : h + 1, :]
    heads_q = spread[...].astype(BF16)
    used = frames_ref[0] - lax.axis_index("s") * FRAMES_HERE
    scores = []
    for j in range(FRAMES_HERE):
        part = lax.dot_general(
            heads_q, tok[FT * j : FT * (j + 1), :], (((1,), (1,)), ((), ())), preferred_element_type=F32
        )
        scores.append(jnp.where(j < used, part * F32(W_H**-0.5), F32(-1e30)))
    score = jnp.concatenate(scores, axis=1)
    top = jnp.max(score, axis=1, keepdims=True)
    frame = lax.broadcasted_iota(jnp.int32, (H, TOK), 1) // FT
    expd = jnp.where(frame < used, jnp.exp(score - top), F32(0.0))
    total = jnp.sum(expd, axis=1, keepdims=True)
    terms = jnp.concatenate(three_terms(expd), axis=0)
    step = 640
    for n in range(D // step):
        cols = slice(step * n, step * (n + 1))
        out = jnp.dot(terms, tok[:, cols], preferred_element_type=F32)
        mixed[:, cols] = (out[2 * H :] + out[H : 2 * H]) + out[:H]
    zl = lax.axis_index("zl")
    members = jnp.int32(0)
    for place, code in enumerate(MEMBERS):
        members = jnp.where(zl == place, jnp.int32(code), members)
    for k in range(CHUNKS):
        member = (members >> (3 * (k // 2))) & 7
        parts_ref[2 * member + k % 2, :, 0:ROWS] = mixed[:, ROWS * k : ROWS * (k + 1)]
    lane = lax.broadcasted_iota(jnp.int32, (H, 128), 1)
    head = lax.broadcasted_iota(jnp.int32, (H, 128), 0)
    row = jnp.where(lane == 64 + head, top, 0.0) + jnp.where(lane == 80 + head, total, 0.0)
    state_ref[...] = jnp.broadcast_to(jnp.sum(row, axis=0, keepdims=True), (8, 128))


def pool(frames, query, tokens):
    return pl.pallas_call(
        pool_kernel,
        out_shape=(
            jax.ShapeDtypeStruct((CHUNKS, H, 256), F32),
            jax.ShapeDtypeStruct((8, 128), F32),
        ),
        in_specs=[
            pl.BlockSpec(memory_space=pltpu.SMEM),
            pl.BlockSpec(memory_space=pltpu.VMEM),
            pl.BlockSpec(memory_space=pltpu.VMEM),
        ],
        out_specs=(pl.BlockSpec(memory_space=pltpu.VMEM), pl.BlockSpec(memory_space=pltpu.VMEM)),
        scratch_shapes=[
            pltpu.VMEM((H, D), F32),
            pltpu.VMEM((H, D), F32),
        ],
        compiler_params=pltpu.CompilerParams(vmem_limit_bytes=VMEM_LIMIT),
        cost_estimate=pl.CostEstimate(flops=4 * 64 * TOK * D, bytes_accessed=TOK * D * 2, transcendentals=H * TOK),
        name="pool",
    )(frames, query, tokens)


def project_kernel(parts_ref, weight_ref, out_ref):
    x = parts_ref[...].reshape(CHUNKS * H, 256)[:, :ROWS]
    first, second, third = three_terms(x)
    weight = weight_ref[...]
    own = lax.broadcasted_iota(jnp.int32, (H, 256), 0)
    lane = lax.broadcasted_iota(jnp.int32, (H, 256), 1)
    for n in range(E // 256):
        w = weight[:, 256 * n : 256 * (n + 1)]
        y = jnp.dot(third, w, preferred_element_type=F32)
        y = y + jnp.dot(second, w, preferred_element_type=F32)
        y = y + jnp.dot(first, w, preferred_element_type=F32)
        mine = (lane + 256 * n) // W_E == own
        y = jnp.where(mine[None], y.reshape(CHUNKS, H, 256), 0.0)
        y = jnp.sum(y, axis=1)
        out_ref[:, 2 * n, :] = y[:, :128]
        out_ref[:, 2 * n + 1, :] = y[:, 128:]
    zero = jnp.zeros((CHUNKS, 128), F32)
    out_ref[:, 6, :] = zero
    out_ref[:, 7, :] = zero


def project(parts, weight):
    return pl.pallas_call(
        project_kernel,
        out_shape=jax.ShapeDtypeStruct((CHUNKS, 8, 128), F32),
        in_specs=[pl.BlockSpec(memory_space=pltpu.VMEM)] * 2,
        out_specs=pl.BlockSpec(memory_space=pltpu.VMEM),
        compiler_params=pltpu.CompilerParams(vmem_limit_bytes=VMEM_LIMIT),
        name="project",
    )(parts, weight)


def share_kernel(sums_ref, state_ref, text_ref, out_ref):
    total = jnp.sum(sums_ref[...], axis=0)
    text = text_ref[...]
    s = lax.axis_index("s")
    quarter = text[:, 0:192]
    for q in range(1, 4):
        quarter = jnp.where(s == q, text[:, 192 * q : 192 * (q + 1)], quarter)
    lane = lax.broadcasted_iota(jnp.int32, (1, 128), 1)
    tail = jnp.concatenate([quarter[:, 128:192], jnp.zeros((1, 64), F32)], axis=1)
    tail = jnp.where(lane < 64, tail, state_ref[0:1, :])
    row = lax.broadcasted_iota(jnp.int32, (8, 128), 0)
    block = jnp.where(row < 6, total, jnp.where(row == 6, quarter[:, 0:128], tail))
    out_ref[...] = jnp.broadcast_to(block[None], out_ref.shape)


def share(sums, state, text):
    return pl.pallas_call(
        share_kernel,
        out_shape=jax.ShapeDtypeStruct((32, 8, 128), F32),
        in_specs=[pl.BlockSpec(memory_space=pltpu.VMEM)] * 3,
        out_specs=pl.BlockSpec(memory_space=pltpu.VMEM),
        compiler_params=pltpu.CompilerParams(vmem_limit_bytes=VMEM_LIMIT),
        name="share",
    )(sums, state, text)


def unit_rows(values):
    return values * lax.rsqrt(jnp.sum(values * values, axis=1, keepdims=True) + 1e-06)


def merge_kernel(parts_ref, out_ref, video_ref, rows):
    ends = [parts_ref[8 * s : 8 * (s + 1), 7, :] for s in range(4)]
    tops = [end[:, 64 : 64 + H] for end in ends]
    totals = [end[:, 80 : 80 + H] for end in ends]
    top = jnp.maximum(jnp.maximum(tops[0], tops[1]), jnp.maximum(tops[2], tops[3]))
    scales = [jnp.exp(t - top) for t in tops]
    total = sum(scale * value for scale, value in zip(scales, totals))
    scales = jnp.concatenate([scale / total for scale in scales], axis=0)
    lane = lax.broadcasted_iota(jnp.int32, (H, E), 1) // W_E
    head = lax.broadcasted_iota(jnp.int32, (H, E), 0)
    spread = jnp.where(lane == head, F32(1.0), F32(0.0))
    factors = jnp.dot(scales, spread, precision=HIGH, preferred_element_type=F32)
    pooled = jnp.zeros((8, E), F32)
    texts = []
    for s in range(4):
        mine = [parts_ref[8 * s : 8 * (s + 1), r, :] for r in range(6)]
        pooled = pooled + factors[8 * s : 8 * (s + 1)] * jnp.concatenate(mine, axis=1)
        texts += [parts_ref[8 * s : 8 * (s + 1), 6, :], ends[s][:, 0:64]]
    videos = unit_rows(pooled)
    texts = unit_rows(jnp.concatenate(texts, axis=1))
    out_ref[:, 0:8, :] = jnp.broadcast_to(videos[None], (16, 8, E))
    out_ref[:, 8:16, :] = jnp.broadcast_to(texts[None], (16, 8, E))
    rows[...] = videos
    video_ref[...] = rows[pl.ds(lax.axis_index("zl"), 1), :]


def merge(parts):
    return pl.pallas_call(
        merge_kernel,
        out_shape=(jax.ShapeDtypeStruct((16, 16, E), F32), jax.ShapeDtypeStruct((1, E), F32)),
        in_specs=[pl.BlockSpec(memory_space=pltpu.VMEM)],
        out_specs=(pl.BlockSpec(memory_space=pltpu.VMEM), pl.BlockSpec(memory_space=pltpu.VMEM)),
        scratch_shapes=[pltpu.VMEM((8, E), F32)],
        compiler_params=pltpu.CompilerParams(vmem_limit_bytes=VMEM_LIMIT),
        name="merge",
    )(parts)


def loss_kernel(scale_ref, pair_ref, mine_ref, other_ref, video_ref, text_ref, loss_ref, videos, texts, grads):
    core = lax.axis_index("c")
    here = lax.axis_index("xh") * 2 + lax.axis_index("xl")
    place = (here * 4 + lax.axis_index("y")) * 8 + lax.axis_index("zl")
    n = 256
    for ref, start in ((mine_ref, core * 128), (other_ref, (1 - core) * 128)):
        start = pl.multiple_of(start, 128)
        videos[pl.ds(start, 128), :] = ref[:, 0:8, :].reshape(128, E)
        texts[pl.ds(start, 128), :] = ref[:, 8:16, :].reshape(128, E)
    v, t = videos[...], texts[...]
    scale = scale_ref[0]
    logits = scale * lax.dot_general(
        v, t, (((1,), (1,)), ((), ())), precision=HIGH, preferred_element_type=F32
    )
    expd = jnp.exp(logits)
    row_sum = jnp.sum(expd, axis=1, keepdims=True)
    col_sum = jnp.sum(expd, axis=0, keepdims=True)
    row = lax.broadcasted_iota(jnp.int32, (n, n), 0)
    col = lax.broadcasted_iota(jnp.int32, (n, n), 1)
    row_id = 2 * (row % 128) + row // 128
    col_id = 2 * (col % 128) + col // 128
    pairs = jnp.sum(jnp.where(col == row_id, pair_ref[...].astype(F32), 0.0), axis=1, keepdims=True)
    hot = pairs == col_id.astype(F32)
    positive = jnp.sum(jnp.where(hot, logits, 0.0))
    loss_ref[0, 0] = (jnp.sum(jnp.log(row_sum)) + jnp.sum(jnp.log(col_sum)) - 2.0 * positive) / (2.0 * n)
    grad = (expd / row_sum + expd / col_sum - jnp.where(hot, F32(2.0), F32(0.0))) / (2.0 * n)
    grads[...] = grad
    own = core * 128 + place
    own_row = jnp.broadcast_to(grads[pl.ds(own, 1), :], (8, n))
    video_ref[...] = scale * jnp.dot(own_row, t, precision=HIGH, preferred_element_type=F32)[0:1, :]
    own_col = jnp.sum(jnp.where(col == own, grad, 0.0), axis=1, keepdims=True)
    text_ref[...] = scale * jnp.sum(own_col * v, axis=0, keepdims=True)


def losses(scale, pair, mine, other):
    vmem, smem = pl.BlockSpec(memory_space=pltpu.VMEM), pl.BlockSpec(memory_space=pltpu.SMEM)
    return pl.pallas_call(
        loss_kernel,
        out_shape=(
            jax.ShapeDtypeStruct((1, E), F32),
            jax.ShapeDtypeStruct((1, E), F32),
            jax.ShapeDtypeStruct((1, 1), F32),
        ),
        in_specs=[smem, vmem, vmem, vmem],
        out_specs=(vmem, vmem, smem),
        scratch_shapes=[pltpu.VMEM((256, E), F32), pltpu.VMEM((256, E), F32), pltpu.VMEM((256, 256), F32)],
        compiler_params=pltpu.CompilerParams(vmem_limit_bytes=VMEM_LIMIT),
        name="losses",
    )(scale, pair, mine, other)


def exchange(value, axes):
    return lax.all_to_all(value, axes, 0, 0, tiled=True)


def shards(tokens, query, value_weight, frames, text_feat, pair, logit_scale):
    moves = []
    for m in range(8):
        for z in range(32):
            source = (z + HOPS[m][z % 8]) % 32
            moves.append(((8 * m + source % 8) * 4 + source // 8, (8 * m + z % 8) * 4 + z // 8))
    weight = lax.ppermute(value_weight, ("xl", "y", "zl", "s"), moves)
    parts, state = pool(frames, query, tokens)
    parts = exchange(parts, GROUP)
    sums = exchange(project(parts, weight), GROUP)
    gathered = exchange(share(sums, state, text_feat), ("s", "zl"))
    block, video_embed = merge(gathered)
    mine = exchange(block, ("xh", "xl", "y"))
    other = lax.ppermute(mine, "c", [(0, 1), (1, 0)])
    grad_video, grad_text, loss = losses(logit_scale.reshape(1), pair.reshape(1, -1), mine, other)
    return (video_embed, grad_video, grad_text, loss.reshape(()))


def solution(mesh):
    axes = ("xh", "xl", "y", "zl", "c", "s")
    fine = Mesh(mesh.devices.reshape(2, 2, 4, 8, 2, 4), axes)
    clips = axes[:5]
    return jax.shard_map(
        shards,
        mesh=fine,
        in_specs=(
            P(clips, "s", None),
            P(),
            P(("zl", "c"), None),
            P(clips),
            P(clips, None),
            P(),
            P(),
        ),
        out_specs=(P(clips, None), P(clips, None), P(clips, None), P()),
        check_vma=False,
    )
```

```python
import jax
import jax.numpy as jnp
from jax import lax
from jax.experimental import pallas as pl
from jax.experimental.pallas import tpu as pltpu
from jax.sharding import Mesh, PartitionSpec as P

D, E, H, FT = 3200, 768, 16, 128
W_H = D // H
W_E = E // H
CHUNKS = 16
ROWS = D // CHUNKS
TOK = 512
FRAMES_HERE = TOK // FT
HIGH = lax.Precision.HIGHEST
F32, BF16 = jnp.float32, jnp.bfloat16
VMEM_LIMIT = 40 * 1024 * 1024
GROUP = ("xl", "y", "c")


PAIRS = (
    (3, 6, 1, 4, 0, 2, 5, 7),
    (5, 0, 4, 3, 7, 1, 6, 2),
    (0, 7, 3, 6, 1, 4, 2, 5),
    (4, 5, 2, 1, 6, 3, 7, 0),
    (1, 4, 7, 2, 5, 0, 3, 6),
    (6, 3, 0, 5, 2, 7, 4, 1),
    (2, 1, 6, 7, 4, 5, 0, 3),
    (7, 2, 5, 0, 3, 6, 1, 4),
)
HOPS = (
    (3, -3, -1, 1, 4, -3, -1, 0),
    (-3, -1, 2, 0, 3, -4, 0, 3),
    (0, -2, 1, 3, -3, -1, 4, -2),
    (4, -4, 0, -2, 2, -2, 1, 1),
    (1, 3, -3, -1, 1, 3, -3, -1),
    (-2, 2, -2, 2, -2, 2, -2, 2),
    (2, 0, 4, -4, 0, 0, 2, -4),
    (-1, 1, 3, -3, -1, 1, 3, -3),
)
MEMBERS = tuple(sum(m << (3 * PAIRS[m][zl]) for m in range(8)) for zl in range(8))


def three_terms(value):
    first = value.astype(BF16)
    rest = value - first.astype(F32)
    second = rest.astype(BF16)
    third = (rest - second.astype(F32)).astype(BF16)
    return first, second, third


def spread_kernel(query_ref, out_ref, spread):
    spread[...] = jnp.zeros_like(spread)
    rows = query_ref[...].astype(F32)
    for h in range(H):
        spread[h : h + 1, W_H * h : W_H * (h + 1)] = rows[h : h + 1, :]
    out_ref[...] = spread[...].astype(BF16)


def spread_heads(query):
    return pl.pallas_call(
        spread_kernel,
        out_shape=jax.ShapeDtypeStruct((H, D), BF16),
        in_specs=[pl.BlockSpec(memory_space=pltpu.VMEM)],
        out_specs=pl.BlockSpec(memory_space=pltpu.VMEM),
        scratch_shapes=[pltpu.VMEM((H, D), F32)],
        compiler_params=pltpu.CompilerParams(vmem_limit_bytes=VMEM_LIMIT),
        cost_estimate=pl.CostEstimate(flops=10**9, bytes_accessed=10**7, transcendentals=0),
        name="spread_heads",
    )(query)


def pool_kernel(frames_ref, query_ref, tok_ref, parts_ref, state_ref, mixed):
    tok = tok_ref.at[0]
    heads_q = query_ref[...]
    used = frames_ref[0] - lax.axis_index("s") * FRAMES_HERE
    scores = []
    for j in range(FRAMES_HERE):
        part = lax.dot_general(
            heads_q, tok[FT * j : FT * (j + 1), :], (((1,), (1,)), ((), ())), preferred_element_type=F32
        )
        scores.append(jnp.where(j < used, part * F32(W_H**-0.5), F32(-1e30)))
    score = jnp.concatenate(scores, axis=1)
    top = jnp.max(score, axis=1, keepdims=True)
    frame = lax.broadcasted_iota(jnp.int32, (H, TOK), 1) // FT
    expd = jnp.where(frame < used, jnp.exp(score - top), F32(0.0))
    total = jnp.sum(expd, axis=1, keepdims=True)
    terms = jnp.concatenate(three_terms(expd), axis=0)
    step = 640
    for n in range(D // step):
        cols = slice(step * n, step * (n + 1))
        out = jnp.dot(terms, tok[:, cols], preferred_element_type=F32)
        mixed[:, cols] = (out[2 * H :] + out[H : 2 * H]) + out[:H]
    zl = lax.axis_index("zab") * 2 + lax.axis_index("zc")
    members = jnp.int32(0)
    for place, code in enumerate(MEMBERS):
        members = jnp.where(zl == place, jnp.int32(code), members)
    for k in range(CHUNKS):
        member = (members >> (3 * (k // 2))) & 7
        parts_ref[2 * member + k % 2, :, 0:ROWS] = mixed[:, ROWS * k : ROWS * (k + 1)]
    lane = lax.broadcasted_iota(jnp.int32, (H, 128), 1)
    head = lax.broadcasted_iota(jnp.int32, (H, 128), 0)
    row = jnp.where(lane == 64 + head, top, 0.0) + jnp.where(lane == 80 + head, total, 0.0)
    state_ref[...] = jnp.broadcast_to(jnp.sum(row, axis=0, keepdims=True), (8, 128))


def pool(frames, query, tokens):
    return pl.pallas_call(
        pool_kernel,
        out_shape=(
            jax.ShapeDtypeStruct((CHUNKS, H, 256), F32),
            jax.ShapeDtypeStruct((8, 128), F32),
        ),
        in_specs=[
            pl.BlockSpec(memory_space=pltpu.SMEM),
            pl.BlockSpec(memory_space=pltpu.VMEM),
            pl.BlockSpec(memory_space=pltpu.VMEM),
        ],
        out_specs=(pl.BlockSpec(memory_space=pltpu.VMEM), pl.BlockSpec(memory_space=pltpu.VMEM)),
        scratch_shapes=[pltpu.VMEM((H, D), F32)],
        compiler_params=pltpu.CompilerParams(vmem_limit_bytes=VMEM_LIMIT),
        cost_estimate=pl.CostEstimate(flops=4 * 64 * TOK * D, bytes_accessed=TOK * D * 2, transcendentals=H * TOK),
        name="pool",
    )(frames, query, tokens)


def project_kernel(parts_ref, weight_ref, out_ref):
    x = parts_ref[...].reshape(CHUNKS * H, 256)[:, :ROWS]
    first, second, third = three_terms(x)
    weight = weight_ref[...]
    own = lax.broadcasted_iota(jnp.int32, (H, 256), 0)
    lane = lax.broadcasted_iota(jnp.int32, (H, 256), 1)
    for n in range(E // 256):
        w = weight[:, 256 * n : 256 * (n + 1)]
        y = jnp.dot(third, w, preferred_element_type=F32)
        y = y + jnp.dot(second, w, preferred_element_type=F32)
        y = y + jnp.dot(first, w, preferred_element_type=F32)
        mine = (lane + 256 * n) // W_E == own
        y = jnp.where(mine[None], y.reshape(CHUNKS, H, 256), 0.0)
        y = jnp.sum(y, axis=1)
        out_ref[:, 2 * n, :] = y[:, :128]
        out_ref[:, 2 * n + 1, :] = y[:, 128:]
    zero = jnp.zeros((CHUNKS, 128), F32)
    out_ref[:, 6, :] = zero
    out_ref[:, 7, :] = zero


def project(parts, weight):
    return pl.pallas_call(
        project_kernel,
        out_shape=jax.ShapeDtypeStruct((CHUNKS, 8, 128), F32),
        in_specs=[pl.BlockSpec(memory_space=pltpu.VMEM)] * 2,
        out_specs=pl.BlockSpec(memory_space=pltpu.VMEM),
        compiler_params=pltpu.CompilerParams(vmem_limit_bytes=VMEM_LIMIT),
        name="project",
    )(parts, weight)


def share_kernel(sums_ref, state_ref, text_ref, out_ref):
    total = jnp.sum(sums_ref[...], axis=0)
    text = text_ref[...]
    s = lax.axis_index("s")
    quarter = text[:, 0:192]
    for q in range(1, 4):
        quarter = jnp.where(s == q, text[:, 192 * q : 192 * (q + 1)], quarter)
    lane = lax.broadcasted_iota(jnp.int32, (1, 128), 1)
    tail = jnp.concatenate([quarter[:, 128:192], jnp.zeros((1, 64), F32)], axis=1)
    tail = jnp.where(lane < 64, tail, state_ref[0:1, :])
    row = lax.broadcasted_iota(jnp.int32, (8, 128), 0)
    block = jnp.where(row < 6, total, jnp.where(row == 6, quarter[:, 0:128], tail))
    out_ref[...] = jnp.broadcast_to(block[None], out_ref.shape)


def share(sums, state, text):
    return pl.pallas_call(
        share_kernel,
        out_shape=jax.ShapeDtypeStruct((16, 8, 128), F32),
        in_specs=[pl.BlockSpec(memory_space=pltpu.VMEM)] * 3,
        out_specs=pl.BlockSpec(memory_space=pltpu.VMEM),
        compiler_params=pltpu.CompilerParams(vmem_limit_bytes=VMEM_LIMIT),
        name="share",
    )(sums, state, text)


def unit_rows(values):
    return values * lax.rsqrt(jnp.sum(values * values, axis=1, keepdims=True) + 1e-06)


def merge_kernel(parts_ref, out_ref, video_ref, rows):
    ends = [parts_ref[4 * s : 4 * (s + 1), 7, :] for s in range(4)]
    tops = [end[:, 64 : 64 + H] for end in ends]
    totals = [end[:, 80 : 80 + H] for end in ends]
    top = jnp.maximum(jnp.maximum(tops[0], tops[1]), jnp.maximum(tops[2], tops[3]))
    scales = [jnp.exp(t - top) for t in tops]
    total = sum(scale * value for scale, value in zip(scales, totals))
    lane = lax.broadcasted_iota(jnp.int32, (H, E), 1) // W_E
    head = lax.broadcasted_iota(jnp.int32, (H, E), 0)
    spread = jnp.where(lane == head, F32(1.0), F32(0.0))
    factors = jnp.concatenate([scale / total for scale in scales], axis=0)
    factors = jnp.dot(factors, spread, precision=HIGH, preferred_element_type=F32)
    pooled = jnp.zeros((4, E), F32)
    texts = []
    for s in range(4):
        mine = [parts_ref[4 * s : 4 * (s + 1), r, :] for r in range(6)]
        pooled = pooled + factors[4 * s : 4 * (s + 1)] * jnp.concatenate(mine, axis=1)
        texts += [parts_ref[4 * s : 4 * (s + 1), 6, :], ends[s][:, 0:64]]
    videos = unit_rows(pooled)
    texts = unit_rows(jnp.concatenate(texts, axis=1))
    rows[0:4, :] = videos
    rows[4:8, :] = texts
    out_ref[...] = jnp.broadcast_to(rows[...][None], (32, 8, E)).reshape(256, E)
    video_ref[...] = rows[pl.ds(lax.axis_index("zab"), 1), :]


def merge(parts):
    return pl.pallas_call(
        merge_kernel,
        out_shape=(jax.ShapeDtypeStruct((256, E), F32), jax.ShapeDtypeStruct((1, E), F32)),
        in_specs=[pl.BlockSpec(memory_space=pltpu.VMEM)],
        out_specs=(pl.BlockSpec(memory_space=pltpu.VMEM), pl.BlockSpec(memory_space=pltpu.VMEM)),
        scratch_shapes=[pltpu.VMEM((8, E), F32)],
        compiler_params=pltpu.CompilerParams(vmem_limit_bytes=VMEM_LIMIT),
        name="merge",
    )(parts)


def clip_of(row):
    return (row % 128 // 8) * 16 + (row % 4) * 4 + (row // 4 % 2) * 2 + row // 128


def loss_kernel(scale_ref, pair_ref, mine_ref, other_ref, video_ref, text_ref, loss_ref, videos, texts, grads):
    core = lax.axis_index("c")
    here = lax.axis_index("xh") * 2 + lax.axis_index("xl")
    place = ((here * 4 + lax.axis_index("y")) * 2 + lax.axis_index("zc")) * 4 + lax.axis_index("zab")
    n = 256
    for ref, start in ((mine_ref, core * 128), (other_ref, (1 - core) * 128)):
        start = pl.multiple_of(start, 128)
        blocks = ref[...].reshape(16, 2, 8, E)
        even, odd = blocks[:, 0], blocks[:, 1]
        low = lax.broadcasted_iota(jnp.int32, (16, 8, E), 1) < 4
        videos[pl.ds(start, 128), :] = jnp.where(low, even, pltpu.roll(odd, 4, 1)).reshape(128, E)
        texts[pl.ds(start, 128), :] = jnp.where(low, pltpu.roll(even, 4, 1), odd).reshape(128, E)
    v, t = videos[...], texts[...]
    scale = scale_ref[0]
    logits = scale * lax.dot_general(
        v, t, (((1,), (1,)), ((), ())), precision=HIGH, preferred_element_type=F32
    )
    expd = jnp.exp(logits)
    row_sum = jnp.sum(expd, axis=1, keepdims=True)
    col_sum = jnp.sum(expd, axis=0, keepdims=True)
    row = lax.broadcasted_iota(jnp.int32, (n, n), 0)
    col = lax.broadcasted_iota(jnp.int32, (n, n), 1)
    row_id, col_id = clip_of(row), clip_of(col)
    pairs = jnp.sum(jnp.where(col == row_id, pair_ref[...].astype(F32), 0.0), axis=1, keepdims=True)
    hot = pairs == col_id.astype(F32)
    positive = jnp.sum(jnp.where(hot, logits, 0.0))
    loss_ref[0, 0] = (jnp.sum(jnp.log(row_sum)) + jnp.sum(jnp.log(col_sum)) - 2.0 * positive) / (2.0 * n)
    grad = (expd / row_sum + expd / col_sum - jnp.where(hot, F32(2.0), F32(0.0))) / (2.0 * n)
    grads[...] = grad
    own = core * 128 + place
    own_row = jnp.broadcast_to(grads[pl.ds(own, 1), :], (8, n))
    video_ref[...] = scale * jnp.dot(own_row, t, precision=HIGH, preferred_element_type=F32)[0:1, :]
    own_col = jnp.sum(jnp.where(col == own, grad, 0.0), axis=1, keepdims=True)
    text_ref[...] = scale * jnp.sum(own_col * v, axis=0, keepdims=True)


def losses(scale, pair, mine, other):
    vmem, smem = pl.BlockSpec(memory_space=pltpu.VMEM), pl.BlockSpec(memory_space=pltpu.SMEM)
    return pl.pallas_call(
        loss_kernel,
        out_shape=(
            jax.ShapeDtypeStruct((1, E), F32),
            jax.ShapeDtypeStruct((1, E), F32),
            jax.ShapeDtypeStruct((1, 1), F32),
        ),
        in_specs=[smem, vmem, vmem, vmem],
        out_specs=(vmem, vmem, smem),
        scratch_shapes=[pltpu.VMEM((256, E), F32), pltpu.VMEM((256, E), F32), pltpu.VMEM((256, 256), F32)],
        compiler_params=pltpu.CompilerParams(vmem_limit_bytes=VMEM_LIMIT),
        name="losses",
    )(scale, pair, mine, other)


def exchange(value, axes):
    return lax.all_to_all(value, axes, 0, 0, tiled=True)


def shards(tokens, query, value_weight, frames, text_feat, pair, logit_scale):
    moves = []
    for m in range(8):
        for z in range(32):
            source = (z + HOPS[m][z % 8]) % 32
            moves.append(((8 * m + source % 8) * 4 + source // 8, (8 * m + z % 8) * 4 + z // 8))
    heads_q = spread_heads(query)
    value_weight, heads_q = lax.optimization_barrier((value_weight, heads_q))
    weight = lax.ppermute(value_weight, ("xl", "y", "zab", "zc", "s"), moves)
    parts, state = pool(frames, heads_q, tokens)
    parts = exchange(parts, GROUP)
    sums = exchange(project(parts, weight), GROUP)
    gathered = exchange(share(sums, state, text_feat), ("s", "zab"))
    block, video_embed = merge(gathered)
    mine = exchange(block, ("xh", "xl", "y", "zc"))
    other = lax.ppermute(mine, "c", [(0, 1), (1, 0)])
    grad_video, grad_text, loss = losses(logit_scale.reshape(1), pair.reshape(1, -1), mine, other)
    return (video_embed, grad_video, grad_text, loss.reshape(()))


def solution(mesh):
    axes = ("xh", "xl", "y", "zab", "zc", "c", "s")
    fine = Mesh(mesh.devices.reshape(2, 2, 4, 4, 2, 2, 4), axes)
    clips = axes[:6]
    return jax.shard_map(
        shards,
        mesh=fine,
        in_specs=(
            P(clips, "s", None),
            P(),
            P(("zab", "zc", "c"), None),
            P(clips),
            P(clips, None),
            P(),
            P(),
        ),
        out_specs=(P(clips, None), P(clips, None), P(clips, None), P()),
        check_vma=False,
    )
```

```python
import jax
import jax.numpy as jnp
from jax import lax
from jax.experimental import pallas as pl
from jax.experimental.pallas import tpu as pltpu
from jax.sharding import Mesh, PartitionSpec as P

D, E, H, FT = 3200, 768, 16, 128
W_H = D // H
W_E = E // H
CHUNKS = 16
ROWS = D // CHUNKS
TOK = 512
FRAMES_HERE = TOK // FT
HIGH = lax.Precision.HIGHEST
F32, BF16 = jnp.float32, jnp.bfloat16
VMEM_LIMIT = 40 * 1024 * 1024
GROUP = ("xl", "y", "c")


PAIRS = (
    (3, 6, 1, 4, 0, 2, 5, 7),
    (5, 0, 4, 3, 7, 1, 6, 2),
    (0, 7, 3, 6, 1, 4, 2, 5),
    (4, 5, 2, 1, 6, 3, 7, 0),
    (1, 4, 7, 2, 5, 0, 3, 6),
    (6, 3, 0, 5, 2, 7, 4, 1),
    (2, 1, 6, 7, 4, 5, 0, 3),
    (7, 2, 5, 0, 3, 6, 1, 4),
)
HOPS = (
    (3, -3, -1, 1, 4, -3, -1, 0),
    (-3, -1, 2, 0, 3, -4, 0, 3),
    (0, -2, 1, 3, -3, -1, 4, -2),
    (4, -4, 0, -2, 2, -2, 1, 1),
    (1, 3, -3, -1, 1, 3, -3, -1),
    (-2, 2, -2, 2, -2, 2, -2, 2),
    (2, 0, 4, -4, 0, 0, 2, -4),
    (-1, 1, 3, -3, -1, 1, 3, -3),
)
MEMBERS = tuple(sum(m << (3 * PAIRS[m][zl]) for m in range(8)) for zl in range(8))


def three_terms(value):
    first = value.astype(BF16)
    rest = value - first.astype(F32)
    second = rest.astype(BF16)
    third = (rest - second.astype(F32)).astype(BF16)
    return first, second, third


def used_kernel(frames_ref, out_ref):
    out_ref[...] = jnp.full((8, 128), frames_ref[0] - lax.axis_index("s") * FRAMES_HERE, jnp.int32)


def used_frames(frames):
    return pl.pallas_call(
        used_kernel,
        out_shape=jax.ShapeDtypeStruct((8, 128), jnp.int32),
        in_specs=[pl.BlockSpec(memory_space=pltpu.SMEM)],
        out_specs=pl.BlockSpec(memory_space=pltpu.VMEM),
        compiler_params=pltpu.CompilerParams(vmem_limit_bytes=1024 * 1024),
        cost_estimate=pl.CostEstimate(flops=10**9, bytes_accessed=10**7, transcendentals=0),
        name="used_frames",
    )(frames)


def pool_kernel(used_ref, query_ref, tok_ref, parts_ref, state_ref, spread, mixed):
    tok = tok_ref.at[0]
    spread[...] = jnp.zeros_like(spread)
    rows = query_ref[...].astype(F32)
    for h in range(H):
        spread[h : h + 1, W_H * h : W_H * (h + 1)] = rows[h : h + 1, :]
    heads_q = spread[...].astype(BF16)
    used = used_ref[0:1, 0:1]
    scores = []
    for j in range(FRAMES_HERE):
        part = lax.dot_general(
            heads_q, tok[FT * j : FT * (j + 1), :], (((1,), (1,)), ((), ())), preferred_element_type=F32
        )
        scores.append(jnp.where(j < used, part * F32(W_H**-0.5), F32(-1e30)))
    score = jnp.concatenate(scores, axis=1)
    top = jnp.max(score, axis=1, keepdims=True)
    frame = lax.broadcasted_iota(jnp.int32, (H, TOK), 1) // FT
    expd = jnp.where(frame < used, jnp.exp(score - top), F32(0.0))
    total = jnp.sum(expd, axis=1, keepdims=True)
    terms = jnp.concatenate(three_terms(expd), axis=0)
    step = 640
    for n in range(D // step):
        cols = slice(step * n, step * (n + 1))
        out = jnp.dot(terms, tok[:, cols], preferred_element_type=F32)
        mixed[:, cols] = (out[2 * H :] + out[H : 2 * H]) + out[:H]
    zl = lax.axis_index("zab") * 2 + lax.axis_index("zc")
    members = jnp.int32(0)
    for place, code in enumerate(MEMBERS):
        members = jnp.where(zl == place, jnp.int32(code), members)
    for k in range(CHUNKS):
        member = (members >> (3 * (k // 2))) & 7
        parts_ref[2 * member + k % 2, :, 0:ROWS] = mixed[:, ROWS * k : ROWS * (k + 1)]
    lane = lax.broadcasted_iota(jnp.int32, (H, 128), 1)
    head = lax.broadcasted_iota(jnp.int32, (H, 128), 0)
    row = jnp.where(lane == 64 + head, top, 0.0) + jnp.where(lane == 80 + head, total, 0.0)
    state_ref[...] = jnp.broadcast_to(jnp.sum(row, axis=0, keepdims=True), (8, 128))


def pool(used, query, tokens):
    return pl.pallas_call(
        pool_kernel,
        out_shape=(
            jax.ShapeDtypeStruct((CHUNKS, H, 256), F32),
            jax.ShapeDtypeStruct((8, 128), F32),
        ),
        in_specs=[
            pl.BlockSpec(memory_space=pltpu.VMEM),
            pl.BlockSpec(memory_space=pltpu.VMEM),
            pl.BlockSpec(memory_space=pltpu.VMEM),
        ],
        out_specs=(pl.BlockSpec(memory_space=pltpu.VMEM), pl.BlockSpec(memory_space=pltpu.VMEM)),
        scratch_shapes=[pltpu.VMEM((H, D), F32), pltpu.VMEM((H, D), F32)],
        compiler_params=pltpu.CompilerParams(vmem_limit_bytes=VMEM_LIMIT),
        cost_estimate=pl.CostEstimate(flops=4 * 64 * TOK * D, bytes_accessed=TOK * D * 2, transcendentals=H * TOK),
        name="pool",
    )(used, query, tokens)


def project_kernel(parts_ref, weight_ref, out_ref):
    x = parts_ref[...].reshape(CHUNKS * H, 256)[:, :ROWS]
    first, second, third = three_terms(x)
    weight = weight_ref[...]
    own = lax.broadcasted_iota(jnp.int32, (H, 256), 0)
    lane = lax.broadcasted_iota(jnp.int32, (H, 256), 1)
    for n in range(E // 256):
        w = weight[:, 256 * n : 256 * (n + 1)]
        y = jnp.dot(third, w, preferred_element_type=F32)
        y = y + jnp.dot(second, w, preferred_element_type=F32)
        y = y + jnp.dot(first, w, preferred_element_type=F32)
        mine = (lane + 256 * n) // W_E == own
        y = jnp.where(mine[None], y.reshape(CHUNKS, H, 256), 0.0)
        y = jnp.sum(y, axis=1)
        out_ref[:, 2 * n, :] = y[:, :128]
        out_ref[:, 2 * n + 1, :] = y[:, 128:]
    zero = jnp.zeros((CHUNKS, 128), F32)
    out_ref[:, 6, :] = zero
    out_ref[:, 7, :] = zero


def project(parts, weight):
    return pl.pallas_call(
        project_kernel,
        out_shape=jax.ShapeDtypeStruct((CHUNKS, 8, 128), F32),
        in_specs=[pl.BlockSpec(memory_space=pltpu.VMEM)] * 2,
        out_specs=pl.BlockSpec(memory_space=pltpu.VMEM),
        compiler_params=pltpu.CompilerParams(vmem_limit_bytes=VMEM_LIMIT),
        name="project",
    )(parts, weight)


def share_kernel(sums_ref, state_ref, text_ref, out_ref):
    total = jnp.sum(sums_ref[...], axis=0)
    text = text_ref[...]
    s = lax.axis_index("s")
    quarter = text[:, 0:192]
    for q in range(1, 4):
        quarter = jnp.where(s == q, text[:, 192 * q : 192 * (q + 1)], quarter)
    lane = lax.broadcasted_iota(jnp.int32, (1, 128), 1)
    tail = jnp.concatenate([quarter[:, 128:192], jnp.zeros((1, 64), F32)], axis=1)
    tail = jnp.where(lane < 64, tail, state_ref[0:1, :])
    row = lax.broadcasted_iota(jnp.int32, (8, 128), 0)
    block = jnp.where(row < 6, total, jnp.where(row == 6, quarter[:, 0:128], tail))
    out_ref[...] = jnp.broadcast_to(block[None], out_ref.shape)


def share(sums, state, text):
    return pl.pallas_call(
        share_kernel,
        out_shape=jax.ShapeDtypeStruct((16, 8, 128), F32),
        in_specs=[pl.BlockSpec(memory_space=pltpu.VMEM)] * 3,
        out_specs=pl.BlockSpec(memory_space=pltpu.VMEM),
        compiler_params=pltpu.CompilerParams(vmem_limit_bytes=VMEM_LIMIT),
        name="share",
    )(sums, state, text)


def unit_rows(values):
    return values * lax.rsqrt(jnp.sum(values * values, axis=1, keepdims=True) + 1e-06)


def merge_kernel(parts_ref, out_ref, video_ref, rows):
    ends = [parts_ref[4 * s : 4 * (s + 1), 7, :] for s in range(4)]
    tops = [end[:, 64 : 64 + H] for end in ends]
    totals = [end[:, 80 : 80 + H] for end in ends]
    top = jnp.maximum(jnp.maximum(tops[0], tops[1]), jnp.maximum(tops[2], tops[3]))
    scales = [jnp.exp(t - top) for t in tops]
    total = sum(scale * value for scale, value in zip(scales, totals))
    lane = lax.broadcasted_iota(jnp.int32, (H, E), 1) // W_E
    head = lax.broadcasted_iota(jnp.int32, (H, E), 0)
    spread = jnp.where(lane == head, F32(1.0), F32(0.0)).astype(BF16)
    terms = three_terms(jnp.concatenate([scale / total for scale in scales], axis=0))
    terms = jnp.dot(jnp.concatenate(terms, axis=0), spread, preferred_element_type=F32)
    factors = (terms[32:48] + terms[16:32]) + terms[0:16]
    pooled = jnp.zeros((4, E), F32)
    texts = []
    for s in range(4):
        mine = [parts_ref[4 * s : 4 * (s + 1), r, :] for r in range(6)]
        pooled = pooled + factors[4 * s : 4 * (s + 1)] * jnp.concatenate(mine, axis=1)
        texts += [parts_ref[4 * s : 4 * (s + 1), 6, :], ends[s][:, 0:64]]
    videos = unit_rows(pooled)
    texts = unit_rows(jnp.concatenate(texts, axis=1))
    rows[0:4, :] = videos
    rows[4:8, :] = texts
    out_ref[...] = jnp.broadcast_to(rows[...][None], (32, 8, E)).reshape(256, E)
    video_ref[...] = rows[pl.ds(lax.axis_index("zab"), 1), :]


def merge(parts):
    return pl.pallas_call(
        merge_kernel,
        out_shape=(jax.ShapeDtypeStruct((256, E), F32), jax.ShapeDtypeStruct((1, E), F32)),
        in_specs=[pl.BlockSpec(memory_space=pltpu.VMEM)],
        out_specs=(pl.BlockSpec(memory_space=pltpu.VMEM), pl.BlockSpec(memory_space=pltpu.VMEM)),
        scratch_shapes=[pltpu.VMEM((8, E), F32)],
        compiler_params=pltpu.CompilerParams(vmem_limit_bytes=VMEM_LIMIT),
        name="merge",
    )(parts)


def clip_of(row):
    return (row % 128 // 8) * 16 + (row % 4) * 4 + (row // 4 % 2) * 2 + row // 128


def loss_kernel(scale_ref, pair_ref, mine_ref, other_ref, video_ref, text_ref, loss_ref, videos, texts, grads):
    core = lax.axis_index("c")
    here = lax.axis_index("xh") * 2 + lax.axis_index("xl")
    place = ((here * 4 + lax.axis_index("y")) * 2 + lax.axis_index("zc")) * 4 + lax.axis_index("zab")
    n = 256
    for ref, start in ((mine_ref, core * 128), (other_ref, (1 - core) * 128)):
        start = pl.multiple_of(start, 128)
        blocks = ref[...].reshape(16, 2, 8, E)
        even, odd = blocks[:, 0], blocks[:, 1]
        low = lax.broadcasted_iota(jnp.int32, (16, 8, E), 1) < 4
        videos[pl.ds(start, 128), :] = jnp.where(low, even, pltpu.roll(odd, 4, 1)).reshape(128, E)
        texts[pl.ds(start, 128), :] = jnp.where(low, pltpu.roll(even, 4, 1), odd).reshape(128, E)
    v, t = videos[...], texts[...]
    scale = scale_ref[0]
    logits = scale * lax.dot_general(
        v, t, (((1,), (1,)), ((), ())), precision=HIGH, preferred_element_type=F32
    )
    expd = jnp.exp(logits)
    row_sum = jnp.sum(expd, axis=1, keepdims=True)
    col_sum = jnp.sum(expd, axis=0, keepdims=True)
    row = lax.broadcasted_iota(jnp.int32, (n, n), 0)
    col = lax.broadcasted_iota(jnp.int32, (n, n), 1)
    row_id, col_id = clip_of(row), clip_of(col)
    pairs = jnp.sum(jnp.where(col == row_id, pair_ref[...].astype(F32), 0.0), axis=1, keepdims=True)
    hot = pairs == col_id.astype(F32)
    positive = jnp.sum(jnp.where(hot, logits, 0.0))
    loss_ref[0, 0] = (jnp.sum(jnp.log(row_sum)) + jnp.sum(jnp.log(col_sum)) - 2.0 * positive) / (2.0 * n)
    grad = (expd / row_sum + expd / col_sum - jnp.where(hot, F32(2.0), F32(0.0))) / (2.0 * n)
    grads[...] = grad
    own = core * 128 + place
    own_row = jnp.sum(jnp.where(row == col, grads[pl.ds(own, 1), :], 0.0), axis=1, keepdims=True)
    video_ref[...] = scale * jnp.sum(own_row * t, axis=0, keepdims=True)
    own_col = jnp.sum(jnp.where(col == own, grad, 0.0), axis=1, keepdims=True)
    text_ref[...] = scale * jnp.sum(own_col * v, axis=0, keepdims=True)


def losses(scale, pair, mine, other):
    vmem, smem = pl.BlockSpec(memory_space=pltpu.VMEM), pl.BlockSpec(memory_space=pltpu.SMEM)
    return pl.pallas_call(
        loss_kernel,
        out_shape=(
            jax.ShapeDtypeStruct((1, E), F32),
            jax.ShapeDtypeStruct((1, E), F32),
            jax.ShapeDtypeStruct((1, 1), F32),
        ),
        in_specs=[smem, vmem, vmem, vmem],
        out_specs=(vmem, vmem, smem),
        scratch_shapes=[pltpu.VMEM((256, E), F32), pltpu.VMEM((256, E), F32), pltpu.VMEM((256, 256), F32)],
        compiler_params=pltpu.CompilerParams(vmem_limit_bytes=VMEM_LIMIT),
        name="losses",
    )(scale, pair, mine, other)


def exchange(value, axes):
    return lax.all_to_all(value, axes, 0, 0, tiled=True)


def shards(tokens, query, value_weight, frames, text_feat, pair, logit_scale):
    moves = []
    for m in range(8):
        for z in range(32):
            source = (z + HOPS[m][z % 8]) % 32
            moves.append(((8 * m + source % 8) * 4 + source // 8, (8 * m + z % 8) * 4 + z // 8))
    used = used_frames(frames)
    value_weight, used = lax.optimization_barrier((value_weight, used))
    weight = lax.ppermute(value_weight, ("xl", "y", "zab", "zc", "s"), moves)
    parts, state = pool(used, query, tokens)
    parts = exchange(parts, GROUP)
    sums = exchange(project(parts, weight), GROUP)
    gathered = exchange(share(sums, state, text_feat), ("s", "zab"))
    block, video_embed = merge(gathered)
    mine = exchange(block, ("xh", "xl", "y", "zc"))
    other = lax.ppermute(mine, "c", [(0, 1), (1, 0)])
    grad_video, grad_text, loss = losses(logit_scale.reshape(1), pair.reshape(1, -1), mine, other)
    return (video_embed, grad_video, grad_text, loss.reshape(()))


def solution(mesh):
    axes = ("xh", "xl", "y", "zab", "zc", "c", "s")
    fine = Mesh(mesh.devices.reshape(2, 2, 4, 4, 2, 2, 4), axes)
    clips = axes[:6]
    return jax.shard_map(
        shards,
        mesh=fine,
        in_specs=(
            P(clips, "s", None),
            P(),
            P(("zab", "zc", "c"), None),
            P(clips),
            P(clips, None),
            P(),
            P(),
        ),
        out_specs=(P(clips, None), P(clips, None), P(clips, None), P()),
        check_vma=False,
    )
```

```python
import jax
import jax.numpy as jnp
from jax import lax
from jax.experimental import pallas as pl
from jax.experimental.pallas import tpu as pltpu
from jax.sharding import Mesh, PartitionSpec as P

D, E, H, FT = 3200, 768, 16, 128
W_H = D // H
W_E = E // H
CHUNKS = 16
ROWS = D // CHUNKS
TOK = 512
FRAMES_HERE = TOK // FT
HIGH = lax.Precision.HIGHEST
F32, BF16 = jnp.float32, jnp.bfloat16
VMEM_LIMIT = 40 * 1024 * 1024
GROUP = ("xl", "y", "c")


PAIRS = (
    (3, 6, 1, 4, 0, 2, 5, 7),
    (5, 0, 4, 3, 7, 1, 6, 2),
    (0, 7, 3, 6, 1, 4, 2, 5),
    (4, 5, 2, 1, 6, 3, 7, 0),
    (1, 4, 7, 2, 5, 0, 3, 6),
    (6, 3, 0, 5, 2, 7, 4, 1),
    (2, 1, 6, 7, 4, 5, 0, 3),
    (7, 2, 5, 0, 3, 6, 1, 4),
)
HOPS = (
    (3, -3, -1, 1, 4, -3, -1, 0),
    (-3, -1, 2, 0, 3, -4, 0, 3),
    (0, -2, 1, 3, -3, -1, 4, -2),
    (4, -4, 0, -2, 2, -2, 1, 1),
    (1, 3, -3, -1, 1, 3, -3, -1),
    (-2, 2, -2, 2, -2, 2, -2, 2),
    (2, 0, 4, -4, 0, 0, 2, -4),
    (-1, 1, 3, -3, -1, 1, 3, -3),
)
MEMBERS = tuple(sum(m << (3 * PAIRS[m][zl]) for m in range(8)) for zl in range(8))


def three_terms(value):
    first = value.astype(BF16)
    rest = value - first.astype(F32)
    second = rest.astype(BF16)
    third = (rest - second.astype(F32)).astype(BF16)
    return first, second, third


def used_kernel(frames_ref, out_ref):
    out_ref[...] = jnp.full((8, 128), frames_ref[0] - lax.axis_index("s") * FRAMES_HERE, jnp.int32)


def used_frames(frames):
    return pl.pallas_call(
        used_kernel,
        out_shape=jax.ShapeDtypeStruct((8, 128), jnp.int32),
        in_specs=[pl.BlockSpec(memory_space=pltpu.SMEM)],
        out_specs=pl.BlockSpec(memory_space=pltpu.VMEM),
        compiler_params=pltpu.CompilerParams(vmem_limit_bytes=1024 * 1024),
        cost_estimate=pl.CostEstimate(flops=10**9, bytes_accessed=10**7, transcendentals=0),
        name="used_frames",
    )(frames)


def pool_kernel(used_ref, query_ref, tok_ref, parts_ref, state_ref, spread, mixed):
    tok = tok_ref.at[0]
    spread[...] = jnp.zeros_like(spread)
    rows = query_ref[...].astype(F32)
    for h in range(H):
        spread[h : h + 1, W_H * h : W_H * (h + 1)] = rows[h : h + 1, :]
    heads_q = spread[...].astype(BF16)
    used = used_ref[0:1, 0:1]
    scores = []
    for j in range(FRAMES_HERE):
        part = lax.dot_general(
            heads_q, tok[FT * j : FT * (j + 1), :], (((1,), (1,)), ((), ())), preferred_element_type=F32
        )
        scores.append(jnp.where(j < used, part * F32(W_H**-0.5), F32(-1e30)))
    score = jnp.concatenate(scores, axis=1)
    top = jnp.max(score, axis=1, keepdims=True)
    frame = lax.broadcasted_iota(jnp.int32, (H, TOK), 1) // FT
    expd = jnp.where(frame < used, jnp.exp(score - top), F32(0.0))
    total = jnp.sum(expd, axis=1, keepdims=True)
    terms = jnp.concatenate(three_terms(expd), axis=0)
    step = 640
    for n in range(D // step):
        cols = slice(step * n, step * (n + 1))
        out = jnp.dot(terms, tok[:, cols], preferred_element_type=F32)
        mixed[:, cols] = (out[2 * H :] + out[H : 2 * H]) + out[:H]
    zl = lax.axis_index("zab") * 2 + lax.axis_index("zc")
    members = jnp.int32(0)
    for place, code in enumerate(MEMBERS):
        members = jnp.where(zl == place, jnp.int32(code), members)
    for k in range(CHUNKS):
        member = (members >> (3 * (k // 2))) & 7
        parts_ref[2 * member + k % 2, :, 0:ROWS] = mixed[:, ROWS * k : ROWS * (k + 1)]
    lane = lax.broadcasted_iota(jnp.int32, (H, 128), 1)
    head = lax.broadcasted_iota(jnp.int32, (H, 128), 0)
    row = jnp.where(lane == 64 + head, top, 0.0) + jnp.where(lane == 80 + head, total, 0.0)
    state_ref[...] = jnp.broadcast_to(jnp.sum(row, axis=0, keepdims=True), (8, 128))


def pool(used, query, tokens):
    return pl.pallas_call(
        pool_kernel,
        out_shape=(
            jax.ShapeDtypeStruct((CHUNKS, H, 256), F32),
            jax.ShapeDtypeStruct((8, 128), F32),
        ),
        in_specs=[
            pl.BlockSpec(memory_space=pltpu.VMEM),
            pl.BlockSpec(memory_space=pltpu.VMEM),
            pl.BlockSpec(memory_space=pltpu.VMEM),
        ],
        out_specs=(pl.BlockSpec(memory_space=pltpu.VMEM), pl.BlockSpec(memory_space=pltpu.VMEM)),
        scratch_shapes=[pltpu.VMEM((H, D), F32), pltpu.VMEM((H, D), F32)],
        compiler_params=pltpu.CompilerParams(vmem_limit_bytes=VMEM_LIMIT),
        cost_estimate=pl.CostEstimate(flops=4 * 64 * TOK * D, bytes_accessed=TOK * D * 2, transcendentals=H * TOK),
        name="pool",
    )(used, query, tokens)


def project_kernel(parts_ref, weight_ref, out_ref):
    x = parts_ref[...].reshape(CHUNKS * H, 256)[:, :ROWS]
    first, second, third = three_terms(x)
    weight = weight_ref[...]
    own = lax.broadcasted_iota(jnp.int32, (H, 256), 0)
    lane = lax.broadcasted_iota(jnp.int32, (H, 256), 1)
    for n in range(E // 256):
        w = weight[:, 256 * n : 256 * (n + 1)]
        y = jnp.dot(third, w, preferred_element_type=F32)
        y = y + jnp.dot(second, w, preferred_element_type=F32)
        y = y + jnp.dot(first, w, preferred_element_type=F32)
        mine = (lane + 256 * n) // W_E == own
        y = jnp.where(mine[None], y.reshape(CHUNKS, H, 256), 0.0)
        y = jnp.sum(y, axis=1)
        out_ref[:, 2 * n, :] = y[:, :128]
        out_ref[:, 2 * n + 1, :] = y[:, 128:]
    zero = jnp.zeros((CHUNKS, 128), F32)
    out_ref[:, 6, :] = zero
    out_ref[:, 7, :] = zero


def project(parts, weight):
    return pl.pallas_call(
        project_kernel,
        out_shape=jax.ShapeDtypeStruct((CHUNKS, 8, 128), F32),
        in_specs=[pl.BlockSpec(memory_space=pltpu.VMEM)] * 2,
        out_specs=pl.BlockSpec(memory_space=pltpu.VMEM),
        compiler_params=pltpu.CompilerParams(vmem_limit_bytes=VMEM_LIMIT),
        name="project",
    )(parts, weight)


def share_kernel(sums_ref, state_ref, text_ref, out_ref):
    total = jnp.sum(sums_ref[...], axis=0)
    text = text_ref[...]
    s = lax.axis_index("s")
    quarter = text[:, 0:192]
    for q in range(1, 4):
        quarter = jnp.where(s == q, text[:, 192 * q : 192 * (q + 1)], quarter)
    lane = lax.broadcasted_iota(jnp.int32, (1, 128), 1)
    tail = jnp.concatenate([quarter[:, 128:192], jnp.zeros((1, 64), F32)], axis=1)
    tail = jnp.where(lane < 64, tail, state_ref[0:1, :])
    row = lax.broadcasted_iota(jnp.int32, (8, 128), 0)
    block = jnp.where(row < 6, total, jnp.where(row == 6, quarter[:, 0:128], tail))
    out_ref[...] = jnp.broadcast_to(block[None], out_ref.shape)


def share(sums, state, text):
    return pl.pallas_call(
        share_kernel,
        out_shape=jax.ShapeDtypeStruct((16, 8, 128), F32),
        in_specs=[pl.BlockSpec(memory_space=pltpu.VMEM)] * 3,
        out_specs=pl.BlockSpec(memory_space=pltpu.VMEM),
        compiler_params=pltpu.CompilerParams(vmem_limit_bytes=VMEM_LIMIT),
        name="share",
    )(sums, state, text)


def unit_rows(values):
    return values * lax.rsqrt(jnp.sum(values * values, axis=1, keepdims=True) + 1e-06)


def merge_kernel(parts_ref, out_ref, video_ref, rows):
    own = [pl.ds(s, 4, stride=4) for s in range(4)]
    ends = [parts_ref[own[s], 7, :] for s in range(4)]
    tops = [end[:, 64 : 64 + H] for end in ends]
    totals = [end[:, 80 : 80 + H] for end in ends]
    top = jnp.maximum(jnp.maximum(tops[0], tops[1]), jnp.maximum(tops[2], tops[3]))
    scales = [jnp.exp(t - top) for t in tops]
    total = sum(scale * value for scale, value in zip(scales, totals))
    lane = lax.broadcasted_iota(jnp.int32, (H, E), 1) // W_E
    head = lax.broadcasted_iota(jnp.int32, (H, E), 0)
    spread = jnp.where(lane == head, F32(1.0), F32(0.0)).astype(BF16)
    terms = three_terms(jnp.concatenate([scale / total for scale in scales], axis=0))
    terms = jnp.dot(jnp.concatenate(terms, axis=0), spread, preferred_element_type=F32)
    factors = (terms[32:48] + terms[16:32]) + terms[0:16]
    pooled = jnp.zeros((4, E), F32)
    texts = []
    for s in range(4):
        mine = [parts_ref[own[s], r, :] for r in range(6)]
        pooled = pooled + factors[4 * s : 4 * (s + 1)] * jnp.concatenate(mine, axis=1)
        texts += [parts_ref[own[s], 6, :], ends[s][:, 0:64]]
    videos = unit_rows(pooled)
    texts = unit_rows(jnp.concatenate(texts, axis=1))
    rows[0:4, :] = videos
    rows[4:8, :] = texts
    out_ref[...] = jnp.broadcast_to(rows[...][None], (32, 8, E)).reshape(256, E)
    video_ref[...] = rows[pl.ds(lax.axis_index("zab"), 1), :]


def merge(parts):
    return pl.pallas_call(
        merge_kernel,
        out_shape=(jax.ShapeDtypeStruct((256, E), F32), jax.ShapeDtypeStruct((1, E), F32)),
        in_specs=[pl.BlockSpec(memory_space=pltpu.VMEM)],
        out_specs=(pl.BlockSpec(memory_space=pltpu.VMEM), pl.BlockSpec(memory_space=pltpu.VMEM)),
        scratch_shapes=[pltpu.VMEM((8, E), F32)],
        compiler_params=pltpu.CompilerParams(vmem_limit_bytes=VMEM_LIMIT),
        name="merge",
    )(parts)


def clip_of(row):
    column = (row // 8 % 4) * 4 + row % 128 // 32
    return column * 16 + (row % 4) * 4 + (row // 4 % 2) * 2 + row // 128


def loss_kernel(scale_ref, pair_ref, mine_ref, other_ref, video_ref, text_ref, loss_ref, videos, texts, grads):
    core = lax.axis_index("c")
    here = lax.axis_index("xh") * 2 + lax.axis_index("xl")
    place = ((lax.axis_index("y") * 4 + here) * 2 + lax.axis_index("zc")) * 4 + lax.axis_index("zab")
    n = 256
    for ref, start in ((mine_ref, core * 128), (other_ref, (1 - core) * 128)):
        start = pl.multiple_of(start, 128)
        blocks = ref[...].reshape(16, 2, 8, E)
        even, odd = blocks[:, 0], blocks[:, 1]
        low = lax.broadcasted_iota(jnp.int32, (16, 8, E), 1) < 4
        videos[pl.ds(start, 128), :] = jnp.where(low, even, pltpu.roll(odd, 4, 1)).reshape(128, E)
        texts[pl.ds(start, 128), :] = jnp.where(low, pltpu.roll(even, 4, 1), odd).reshape(128, E)
    v, t = videos[...], texts[...]
    scale = scale_ref[0]
    logits = scale * lax.dot_general(
        v, t, (((1,), (1,)), ((), ())), precision=HIGH, preferred_element_type=F32
    )
    expd = jnp.exp(logits)
    row_sum = jnp.sum(expd, axis=1, keepdims=True)
    col_sum = jnp.sum(expd, axis=0, keepdims=True)
    row = lax.broadcasted_iota(jnp.int32, (n, n), 0)
    col = lax.broadcasted_iota(jnp.int32, (n, n), 1)
    row_id, col_id = clip_of(row), clip_of(col)
    pairs = jnp.sum(jnp.where(col == row_id, pair_ref[...].astype(F32), 0.0), axis=1, keepdims=True)
    hot = pairs == col_id.astype(F32)
    positive = jnp.sum(jnp.where(hot, logits, 0.0))
    loss_ref[0, 0] = (jnp.sum(jnp.log(row_sum)) + jnp.sum(jnp.log(col_sum)) - 2.0 * positive) / (2.0 * n)
    grad = (expd / row_sum + expd / col_sum - jnp.where(hot, F32(2.0), F32(0.0))) / (2.0 * n)
    grads[...] = grad
    own = core * 128 + place
    own_row = jnp.sum(jnp.where(row == col, grads[pl.ds(own, 1), :], 0.0), axis=1, keepdims=True)
    video_ref[...] = scale * jnp.sum(own_row * t, axis=0, keepdims=True)
    own_col = jnp.sum(jnp.where(col == own, grad, 0.0), axis=1, keepdims=True)
    text_ref[...] = scale * jnp.sum(own_col * v, axis=0, keepdims=True)


def losses(scale, pair, mine, other):
    vmem, smem = pl.BlockSpec(memory_space=pltpu.VMEM), pl.BlockSpec(memory_space=pltpu.SMEM)
    return pl.pallas_call(
        loss_kernel,
        out_shape=(
            jax.ShapeDtypeStruct((1, E), F32),
            jax.ShapeDtypeStruct((1, E), F32),
            jax.ShapeDtypeStruct((1, 1), F32),
        ),
        in_specs=[smem, vmem, vmem, vmem],
        out_specs=(vmem, vmem, smem),
        scratch_shapes=[pltpu.VMEM((256, E), F32), pltpu.VMEM((256, E), F32), pltpu.VMEM((256, 256), F32)],
        compiler_params=pltpu.CompilerParams(vmem_limit_bytes=VMEM_LIMIT),
        name="losses",
    )(scale, pair, mine, other)


def exchange(value, axes):
    return lax.all_to_all(value, axes, 0, 0, tiled=True)


def shards(tokens, query, value_weight, frames, text_feat, pair, logit_scale):
    moves = []
    for m in range(8):
        for z in range(32):
            source = (z + HOPS[m][z % 8]) % 32
            moves.append(((8 * m + source % 8) * 4 + source // 8, (8 * m + z % 8) * 4 + z // 8))
    used = used_frames(frames)
    value_weight, used = lax.optimization_barrier((value_weight, used))
    weight = lax.ppermute(value_weight, ("xl", "y", "zab", "zc", "s"), moves)
    parts, state = pool(used, query, tokens)
    parts = exchange(parts, GROUP)
    sums = exchange(project(parts, weight), GROUP)
    gathered = exchange(share(sums, state, text_feat), ("zab", "s"))
    block, video_embed = merge(gathered)
    mine = exchange(block, ("y", "xh", "xl", "zc"))
    other = lax.ppermute(mine, "c", [(0, 1), (1, 0)])
    grad_video, grad_text, loss = losses(logit_scale.reshape(1), pair.reshape(1, -1), mine, other)
    return (video_embed, grad_video, grad_text, loss.reshape(()))


def solution(mesh):
    axes = ("xh", "xl", "y", "zab", "zc", "c", "s")
    fine = Mesh(mesh.devices.reshape(2, 2, 4, 4, 2, 2, 4), axes)
    clips = axes[:6]
    return jax.shard_map(
        shards,
        mesh=fine,
        in_specs=(
            P(clips, "s", None),
            P(),
            P(("zab", "zc", "c"), None),
            P(clips),
            P(clips, None),
            P(),
            P(),
        ),
        out_specs=(P(clips, None), P(clips, None), P(clips, None), P()),
        check_vma=False,
    )
```

```python
import jax
import jax.numpy as jnp
from jax import lax
from jax.experimental import pallas as pl
from jax.experimental.pallas import tpu as pltpu
from jax.sharding import Mesh, PartitionSpec as P

D, E, H, FT = 3200, 768, 16, 128
W_H = D // H
W_E = E // H
CHUNKS = 16
ROWS = D // CHUNKS
TOK = 512
FRAMES_HERE = TOK // FT
HIGH = lax.Precision.HIGHEST
F32, BF16 = jnp.float32, jnp.bfloat16
VMEM_LIMIT = 40 * 1024 * 1024
GROUP = ("c", "xl", "y")


PAIRS = (
    (3, 6, 1, 4, 0, 2, 5, 7),
    (5, 0, 4, 3, 7, 1, 6, 2),
    (0, 7, 3, 6, 1, 4, 2, 5),
    (4, 5, 2, 1, 6, 3, 7, 0),
    (1, 4, 7, 2, 5, 0, 3, 6),
    (6, 3, 0, 5, 2, 7, 4, 1),
    (2, 1, 6, 7, 4, 5, 0, 3),
    (7, 2, 5, 0, 3, 6, 1, 4),
)
HOPS = (
    (3, -3, -1, 1, 4, -3, -1, 0),
    (-3, -1, 2, 0, 3, -4, 0, 3),
    (0, -2, 1, 3, -3, -1, 4, -2),
    (4, -4, 0, -2, 2, -2, 1, 1),
    (1, 3, -3, -1, 1, 3, -3, -1),
    (-2, 2, -2, 2, -2, 2, -2, 2),
    (2, 0, 4, -4, 0, 0, 2, -4),
    (-1, 1, 3, -3, -1, 1, 3, -3),
)
MEMBERS = tuple(sum(m << (3 * PAIRS[m][zl]) for m in range(8)) for zl in range(8))


def three_terms(value):
    first = value.astype(BF16)
    rest = value - first.astype(F32)
    second = rest.astype(BF16)
    third = (rest - second.astype(F32)).astype(BF16)
    return first, second, third


def used_kernel(frames_ref, out_ref):
    out_ref[...] = jnp.full((8, 128), frames_ref[0] - lax.axis_index("s") * FRAMES_HERE, jnp.int32)


def used_frames(frames):
    return pl.pallas_call(
        used_kernel,
        out_shape=jax.ShapeDtypeStruct((8, 128), jnp.int32),
        in_specs=[pl.BlockSpec(memory_space=pltpu.SMEM)],
        out_specs=pl.BlockSpec(memory_space=pltpu.VMEM),
        compiler_params=pltpu.CompilerParams(vmem_limit_bytes=1024 * 1024),
        cost_estimate=pl.CostEstimate(flops=10**9, bytes_accessed=10**7, transcendentals=0),
        name="used_frames",
    )(frames)


def pool_kernel(used_ref, query_ref, tok_ref, parts_ref, state_ref, spread, mixed):
    tok = tok_ref.at[0]
    spread[...] = jnp.zeros_like(spread)
    rows = query_ref[...].astype(F32)
    for h in range(H):
        spread[h : h + 1, W_H * h : W_H * (h + 1)] = rows[h : h + 1, :]
    heads_q = spread[...].astype(BF16)
    used = used_ref[0:1, 0:1]
    scores = []
    for j in range(FRAMES_HERE):
        part = lax.dot_general(
            heads_q, tok[FT * j : FT * (j + 1), :], (((1,), (1,)), ((), ())), preferred_element_type=F32
        )
        scores.append(jnp.where(j < used, part * F32(W_H**-0.5), F32(-1e30)))
    score = jnp.concatenate(scores, axis=1)
    top = jnp.max(score, axis=1, keepdims=True)
    frame = lax.broadcasted_iota(jnp.int32, (H, TOK), 1) // FT
    expd = jnp.where(frame < used, jnp.exp(score - top), F32(0.0))
    total = jnp.sum(expd, axis=1, keepdims=True)
    terms = jnp.concatenate(three_terms(expd), axis=0)
    step = 640
    for n in range(D // step):
        cols = slice(step * n, step * (n + 1))
        out = jnp.dot(terms, tok[:, cols], preferred_element_type=F32)
        mixed[:, cols] = (out[2 * H :] + out[H : 2 * H]) + out[:H]
    zl = lax.axis_index("zab") * 2 + lax.axis_index("zc")
    members = jnp.int32(0)
    for place, code in enumerate(MEMBERS):
        members = jnp.where(zl == place, jnp.int32(code), members)
    for k in range(CHUNKS):
        member = (members >> (3 * (k // 2))) & 7
        parts_ref[8 * (k % 2) + member, :, 0:ROWS] = mixed[:, ROWS * k : ROWS * (k + 1)]
    lane = lax.broadcasted_iota(jnp.int32, (H, 128), 1)
    head = lax.broadcasted_iota(jnp.int32, (H, 128), 0)
    row = jnp.where(lane == 64 + head, top, 0.0) + jnp.where(lane == 80 + head, total, 0.0)
    state_ref[...] = jnp.broadcast_to(jnp.sum(row, axis=0, keepdims=True), (8, 128))


def pool(used, query, tokens):
    return pl.pallas_call(
        pool_kernel,
        out_shape=(
            jax.ShapeDtypeStruct((CHUNKS, H, 256), F32),
            jax.ShapeDtypeStruct((8, 128), F32),
        ),
        in_specs=[
            pl.BlockSpec(memory_space=pltpu.VMEM),
            pl.BlockSpec(memory_space=pltpu.VMEM),
            pl.BlockSpec(memory_space=pltpu.VMEM),
        ],
        out_specs=(pl.BlockSpec(memory_space=pltpu.VMEM), pl.BlockSpec(memory_space=pltpu.VMEM)),
        scratch_shapes=[pltpu.VMEM((H, D), F32), pltpu.VMEM((H, D), F32)],
        compiler_params=pltpu.CompilerParams(vmem_limit_bytes=VMEM_LIMIT),
        cost_estimate=pl.CostEstimate(flops=4 * 64 * TOK * D, bytes_accessed=TOK * D * 2, transcendentals=H * TOK),
        name="pool",
    )(used, query, tokens)


def project_kernel(parts_ref, weight_ref, out_ref):
    x = parts_ref[...].reshape(CHUNKS * H, 256)[:, :ROWS]
    first, second, third = three_terms(x)
    weight = weight_ref[...]
    own = lax.broadcasted_iota(jnp.int32, (H, 256), 0)
    lane = lax.broadcasted_iota(jnp.int32, (H, 256), 1)
    for n in range(E // 256):
        w = weight[:, 256 * n : 256 * (n + 1)]
        y = jnp.dot(third, w, preferred_element_type=F32)
        y = y + jnp.dot(second, w, preferred_element_type=F32)
        y = y + jnp.dot(first, w, preferred_element_type=F32)
        mine = (lane + 256 * n) // W_E == own
        y = jnp.where(mine[None], y.reshape(CHUNKS, H, 256), 0.0)
        y = jnp.sum(y, axis=1)
        out_ref[:, 2 * n, :] = y[:, :128]
        out_ref[:, 2 * n + 1, :] = y[:, 128:]
    zero = jnp.zeros((CHUNKS, 128), F32)
    out_ref[:, 6, :] = zero
    out_ref[:, 7, :] = zero


def project(parts, weight):
    return pl.pallas_call(
        project_kernel,
        out_shape=jax.ShapeDtypeStruct((CHUNKS, 8, 128), F32),
        in_specs=[pl.BlockSpec(memory_space=pltpu.VMEM)] * 2,
        out_specs=pl.BlockSpec(memory_space=pltpu.VMEM),
        compiler_params=pltpu.CompilerParams(vmem_limit_bytes=VMEM_LIMIT),
        name="project",
    )(parts, weight)


def share_kernel(sums_ref, state_ref, text_ref, out_ref):
    total = jnp.sum(sums_ref[...], axis=0)
    text = text_ref[...]
    s = lax.axis_index("s")
    quarter = text[:, 0:192]
    for q in range(1, 4):
        quarter = jnp.where(s == q, text[:, 192 * q : 192 * (q + 1)], quarter)
    lane = lax.broadcasted_iota(jnp.int32, (1, 128), 1)
    tail = jnp.concatenate([quarter[:, 128:192], jnp.zeros((1, 64), F32)], axis=1)
    tail = jnp.where(lane < 64, tail, state_ref[0:1, :])
    row = lax.broadcasted_iota(jnp.int32, (8, 128), 0)
    block = jnp.where(row < 6, total, jnp.where(row == 6, quarter[:, 0:128], tail))
    out_ref[...] = jnp.broadcast_to(block[None], out_ref.shape)


def share(sums, state, text):
    return pl.pallas_call(
        share_kernel,
        out_shape=jax.ShapeDtypeStruct((16, 8, 128), F32),
        in_specs=[pl.BlockSpec(memory_space=pltpu.VMEM)] * 3,
        out_specs=pl.BlockSpec(memory_space=pltpu.VMEM),
        compiler_params=pltpu.CompilerParams(vmem_limit_bytes=VMEM_LIMIT),
        name="share",
    )(sums, state, text)


def unit_rows(values):
    return values * lax.rsqrt(jnp.sum(values * values, axis=1, keepdims=True) + 1e-06)


def merge_kernel(parts_ref, out_ref, video_ref, rows):
    own = [pl.ds(s, 4, stride=4) for s in range(4)]
    ends = [parts_ref[own[s], 7, :] for s in range(4)]
    tops = [end[:, 64 : 64 + H] for end in ends]
    totals = [end[:, 80 : 80 + H] for end in ends]
    top = jnp.maximum(jnp.maximum(tops[0], tops[1]), jnp.maximum(tops[2], tops[3]))
    scales = [jnp.exp(t - top) for t in tops]
    total = sum(scale * value for scale, value in zip(scales, totals))
    lane = lax.broadcasted_iota(jnp.int32, (H, E), 1) // W_E
    head = lax.broadcasted_iota(jnp.int32, (H, E), 0)
    spread = jnp.where(lane == head, F32(1.0), F32(0.0)).astype(BF16)
    terms = three_terms(jnp.concatenate([scale / total for scale in scales], axis=0))
    terms = jnp.dot(jnp.concatenate(terms, axis=0), spread, preferred_element_type=F32)
    factors = (terms[32:48] + terms[16:32]) + terms[0:16]
    pooled = jnp.zeros((4, E), F32)
    texts = []
    for s in range(4):
        mine = [parts_ref[own[s], r, :] for r in range(6)]
        pooled = pooled + factors[4 * s : 4 * (s + 1)] * jnp.concatenate(mine, axis=1)
        texts += [parts_ref[own[s], 6, :], ends[s][:, 0:64]]
    videos = unit_rows(pooled)
    texts = unit_rows(jnp.concatenate(texts, axis=1))
    rows[0:4, :] = videos
    rows[4:8, :] = texts
    out_ref[...] = jnp.broadcast_to(rows[...][None], (32, 8, E)).reshape(256, E)
    video_ref[...] = rows[pl.ds(lax.axis_index("zab"), 1), :]


def merge(parts):
    return pl.pallas_call(
        merge_kernel,
        out_shape=(jax.ShapeDtypeStruct((256, E), F32), jax.ShapeDtypeStruct((1, E), F32)),
        in_specs=[pl.BlockSpec(memory_space=pltpu.VMEM)],
        out_specs=(pl.BlockSpec(memory_space=pltpu.VMEM), pl.BlockSpec(memory_space=pltpu.VMEM)),
        scratch_shapes=[pltpu.VMEM((8, E), F32)],
        compiler_params=pltpu.CompilerParams(vmem_limit_bytes=VMEM_LIMIT),
        name="merge",
    )(parts)


def clip_of(row):
    column = (row // 8 % 4) * 4 + row % 128 // 32
    return column * 16 + (row % 4) * 4 + (row // 4 % 2) * 2 + row // 128


def loss_kernel(scale_ref, pair_ref, mine_ref, other_ref, video_ref, text_ref, loss_ref, videos, texts, grads):
    core = lax.axis_index("c")
    here = lax.axis_index("xh") * 2 + lax.axis_index("xl")
    place = ((lax.axis_index("y") * 4 + here) * 2 + lax.axis_index("zc")) * 4 + lax.axis_index("zab")
    n = 256
    for ref, start in ((mine_ref, core * 128), (other_ref, (1 - core) * 128)):
        start = pl.multiple_of(start, 128)
        blocks = ref[...].reshape(16, 2, 8, E)
        even, odd = blocks[:, 0], blocks[:, 1]
        low = lax.broadcasted_iota(jnp.int32, (16, 8, E), 1) < 4
        videos[pl.ds(start, 128), :] = jnp.where(low, even, pltpu.roll(odd, 4, 1)).reshape(128, E)
        texts[pl.ds(start, 128), :] = jnp.where(low, pltpu.roll(even, 4, 1), odd).reshape(128, E)
    v, t = videos[...], texts[...]
    scale = scale_ref[0]
    logits = scale * lax.dot_general(
        v, t, (((1,), (1,)), ((), ())), precision=HIGH, preferred_element_type=F32
    )
    expd = jnp.exp(logits)
    row_sum = jnp.sum(expd, axis=1, keepdims=True)
    col_sum = jnp.sum(expd, axis=0, keepdims=True)
    row = lax.broadcasted_iota(jnp.int32, (n, n), 0)
    col = lax.broadcasted_iota(jnp.int32, (n, n), 1)
    row_id, col_id = clip_of(row), clip_of(col)
    pairs = jnp.sum(jnp.where(col == row_id, pair_ref[...].astype(F32), 0.0), axis=1, keepdims=True)
    hot = pairs == col_id.astype(F32)
    positive = jnp.sum(jnp.where(hot, logits, 0.0))
    loss_ref[0, 0] = (jnp.sum(jnp.log(row_sum)) + jnp.sum(jnp.log(col_sum)) - 2.0 * positive) / (2.0 * n)
    grad = (expd / row_sum + expd / col_sum - jnp.where(hot, F32(2.0), F32(0.0))) / (2.0 * n)
    grads[...] = grad
    own = core * 128 + place
    own_row = jnp.sum(jnp.where(row == col, grads[pl.ds(own, 1), :], 0.0), axis=1, keepdims=True)
    video_ref[...] = scale * jnp.sum(own_row * t, axis=0, keepdims=True)
    own_col = jnp.sum(jnp.where(col == own, grad, 0.0), axis=1, keepdims=True)
    text_ref[...] = scale * jnp.sum(own_col * v, axis=0, keepdims=True)


def losses(scale, pair, mine, other):
    vmem, smem = pl.BlockSpec(memory_space=pltpu.VMEM), pl.BlockSpec(memory_space=pltpu.SMEM)
    return pl.pallas_call(
        loss_kernel,
        out_shape=(
            jax.ShapeDtypeStruct((1, E), F32),
            jax.ShapeDtypeStruct((1, E), F32),
            jax.ShapeDtypeStruct((1, 1), F32),
        ),
        in_specs=[smem, vmem, vmem, vmem],
        out_specs=(vmem, vmem, smem),
        scratch_shapes=[pltpu.VMEM((256, E), F32), pltpu.VMEM((256, E), F32), pltpu.VMEM((256, 256), F32)],
        compiler_params=pltpu.CompilerParams(vmem_limit_bytes=VMEM_LIMIT),
        name="losses",
    )(scale, pair, mine, other)


def exchange(value, axes):
    return lax.all_to_all(value, axes, 0, 0, tiled=True)


def shards(tokens, query, value_weight, frames, text_feat, pair, logit_scale):
    moves = []
    for m in range(8):
        for z in range(32):
            source = (z + HOPS[m][z % 8]) % 32
            moves.append(((8 * m + source % 8) * 4 + source // 8, (8 * m + z % 8) * 4 + z // 8))
    used = used_frames(frames)
    value_weight, used = lax.optimization_barrier((value_weight, used))
    weight = lax.ppermute(value_weight, ("xl", "y", "zab", "zc", "s"), moves)
    parts, state = pool(used, query, tokens)
    parts = exchange(parts, GROUP)
    sums = exchange(project(parts, weight), GROUP)
    gathered = exchange(share(sums, state, text_feat), ("zab", "s"))
    block, video_embed = merge(gathered)
    mine = exchange(block, ("y", "xh", "xl", "zc"))
    other = lax.ppermute(mine, "c", [(0, 1), (1, 0)])
    grad_video, grad_text, loss = losses(logit_scale.reshape(1), pair.reshape(1, -1), mine, other)
    return (video_embed, grad_video, grad_text, loss.reshape(()))


def solution(mesh):
    axes = ("xh", "xl", "y", "zab", "zc", "c", "s")
    fine = Mesh(mesh.devices.reshape(2, 2, 4, 4, 2, 2, 4), axes)
    clips = axes[:6]
    return jax.shard_map(
        shards,
        mesh=fine,
        in_specs=(
            P(clips, "s", None),
            P(),
            P(("zab", "zc", "c"), None),
            P(clips),
            P(clips, None),
            P(),
            P(),
        ),
        out_specs=(P(clips, None), P(clips, None), P(clips, None), P()),
        check_vma=False,
    )
```
